512 devices in a mesh: space: 8 (over x, core), energy: 64 (over z, y).
Axes of the slice: x: 4, y: 4, z: 16, core: 2. Of those that a mesh axis runs over, the one named last changes fastest.
Arguments:
- lesser_in: bfloat16 [64, 8, 2, 256, 256], P('energy', 'space'), may hold values from -6 to 6
- retarded: bfloat16 [64, 8, 2, 256, 256], P('energy', 'space'), may hold values from -0.25 to 0.25
- coupling: bfloat16 [8, 2, 256, 256], P('space'), may hold values from -0.25 to 0.25
- interaction: bfloat16 [8, 128, 65536], P('space', None, 'energy'), may hold values from -1.5 to 1.5
Outputs:
- self_energy: bfloat16 [64, 8, 2, 256, 256], P('energy', 'space')
The draws below stay inside these ranges and needn't reach their ends.
All inputs are finite; a program needn't handle non-finite values.
Results may differ from the reference program's by a relative error of at most 0.029.
Values may be sent and summed in bfloat16 or wider, within the bound.
No kernel may reach another device: no remote copies, remote signals or barrier semaphores. Data moves between devices by JAX's collectives and lax.ppermute only.
A program may use at most 128 MiB of HBM per device.

```python
import math
import jax
import jax.numpy as jnp
from jax import lax

B = 256
NBLK = 8
NE = 64
NFFT = 128


def level_of(stream_key, extent, split, low, high):
    gain, own = 1.0, jax.random.fold_in(stream_key, 6)
    for axis_at, parts in split:
        heights = jnp.exp(jax.random.uniform(jax.random.fold_in(own, axis_at), (parts,), jnp.float32, low / len(split), high / len(split)))
        gain = gain * jnp.repeat(heights, extent[axis_at] // parts).reshape([-1 if axis == axis_at else 1 for axis in range(len(extent))])
    return gain


def normal_values(key, extent, width, reach, shards=(), kind=jnp.bfloat16):
    values = jax.random.normal(key, extent, jnp.float32) * width
    if len(shards) > 0:
        values = level_of(key, extent, shards, -0.22, 0.18) * values
    return jnp.clip(values, min=-reach, max=reach).astype(kind)


def setup_inputs(seed: int = 0) -> dict:
    key_list = jax.random.split(jax.random.key(seed), 5)
    lesser_in = normal_values(key_list[0], (NE, NBLK, 2, B, B), 1.0, 6.0, ((0, 64), (1, 8)))
    retarded = normal_values(key_list[1], (NE, NBLK, 2, B, B), (2 * B) ** -0.5, 0.25, ((0, 64), (1, 8)))
    coupling = normal_values(key_list[2], (NBLK, 2, B, B), (2 * B + B // 3) ** -0.5, 0.25, ((0, 8),))
    interaction = normal_values(key_list[3], (NBLK, NFFT, B * B), 0.25, 1.5, ((0, 8), (2, 64)))
    return dict(lesser_in=lesser_in, retarded=retarded, coupling=coupling, interaction=interaction)


def product(left_real, left_imag, right_real, right_imag):
    real_part = jnp.dot(left_real, right_real, preferred_element_type=jnp.float32) - jnp.dot(left_imag, right_imag, preferred_element_type=jnp.float32)
    imag_part = jnp.dot(left_real, right_imag, preferred_element_type=jnp.float32) + jnp.dot(left_imag, right_real, preferred_element_type=jnp.float32)
    return real_part, imag_part


def contract(former, latter):
    return lax.dot_general(former, latter, (((1,), (1,)), ((), ())), preferred_element_type=jnp.float32)


def product_adjoint(left_real, left_imag, right_real, right_imag):
    real_part = contract(left_real, right_real) + contract(left_imag, right_imag)
    imag_part = contract(left_imag, right_real) - contract(left_real, right_imag)
    return real_part, imag_part


def phase_table(row_count, column_count, length):
    row_index = jnp.arange(row_count, dtype=jnp.int32)[:, None]
    column_index = jnp.arange(column_count, dtype=jnp.int32)[None, :]
    residue = (row_index * column_index) % length
    return residue.astype(jnp.float32) * (2.0 * math.pi / length)


def finish(spectrum_real, spectrum_imag, weights, energy_count, length):
    forward_scale = energy_count ** -0.5
    inverse_scale = length ** -0.5
    spectrum_real = spectrum_real * forward_scale
    spectrum_imag = spectrum_imag * forward_scale
    weight_values = weights.astype(jnp.float32)
    squared_real = ((spectrum_real * spectrum_real - spectrum_imag * spectrum_imag) * weight_values).astype(jnp.bfloat16)
    squared_imag = (2.0 * spectrum_real * spectrum_imag * weight_values).astype(jnp.bfloat16)
    inverse_phase = phase_table(energy_count, length, length)
    inverse_real = jnp.cos(inverse_phase).astype(jnp.bfloat16)
    inverse_imag = jnp.sin(inverse_phase).astype(jnp.bfloat16)
    out_real, out_imag = product(inverse_real, inverse_imag, squared_real, squared_imag)
    return jnp.stack([out_real * inverse_scale, out_imag * inverse_scale], axis=1).astype(jnp.bfloat16)


def reference(lesser_in, retarded, coupling, interaction):
    block_order = coupling.shape[-1]
    block_count = coupling.shape[0]
    energy_count = lesser_in.shape[0]
    length = 2 * energy_count

    def one_energy(inputs_pair):
        green_in, lesser_here = inputs_pair
        carried_real = jnp.zeros((block_order, block_order), jnp.bfloat16)
        carried_imag = jnp.zeros((block_order, block_order), jnp.bfloat16)
        layers = []
        for block_index in range(block_count):
            resolvent_real = green_in[block_index, 0]
            resolvent_imag = green_in[block_index, 1]
            map_real, map_imag = product(resolvent_real, resolvent_imag, coupling[block_index, 0], coupling[block_index, 1])
            map_real = map_real.astype(jnp.bfloat16)
            map_imag = map_imag.astype(jnp.bfloat16)
            half_real, half_imag = product(resolvent_real, resolvent_imag, lesser_here[block_index, 0], lesser_here[block_index, 1])
            half_real = half_real.astype(jnp.bfloat16)
            half_imag = half_imag.astype(jnp.bfloat16)
            source_real, source_imag = product_adjoint(half_real, half_imag, resolvent_real, resolvent_imag)
            carry_real, carry_imag = product(map_real, map_imag, carried_real, carried_imag)
            carry_real = carry_real.astype(jnp.bfloat16)
            carry_imag = carry_imag.astype(jnp.bfloat16)
            grown_real, grown_imag = product_adjoint(carry_real, carry_imag, map_real, map_imag)
            carried_real = (source_real + grown_real).astype(jnp.bfloat16)
            carried_imag = (source_imag + grown_imag).astype(jnp.bfloat16)
            layers.append(jnp.stack([carried_real, carried_imag]))
        return jnp.stack(layers)

    green_lesser = lax.map(one_energy, (retarded, lesser_in))
    forward_phase = phase_table(length, energy_count, length)
    forward_real = jnp.cos(forward_phase).astype(jnp.bfloat16)
    forward_imag = (-jnp.sin(forward_phase)).astype(jnp.bfloat16)

    def one_block(inputs_pair):
        green_block, weights = inputs_pair
        flattened = green_block.reshape(energy_count, 2, block_order * block_order)
        spectrum_real, spectrum_imag = product(forward_real, forward_imag, flattened[:, 0], flattened[:, 1])
        result = finish(spectrum_real, spectrum_imag, weights, energy_count, length)
        return result.reshape(energy_count, 2, block_order, block_order)

    per_block = lax.map(one_block, (jnp.moveaxis(green_lesser, 1, 0), interaction))
    return jnp.moveaxis(per_block, 0, 1)
```

```python
import math

import jax
import jax.numpy as jnp
from jax import lax
from jax.sharding import Mesh
from jax.sharding import PartitionSpec as P

SPACE = ("chip", "core")
BF16 = jnp.bfloat16
F32 = jnp.float32


def product(left_real, left_imag, right_real, right_imag):
    real_part = jnp.dot(left_real, right_real, preferred_element_type=F32) - jnp.dot(
        left_imag, right_imag, preferred_element_type=F32
    )
    imag_part = jnp.dot(left_real, right_imag, preferred_element_type=F32) + jnp.dot(
        left_imag, right_real, preferred_element_type=F32
    )
    return (real_part, imag_part)


def contract(former, latter):
    return lax.dot_general(former, latter, (((1,), (1,)), ((), ())), preferred_element_type=F32)


def product_adjoint(left_real, left_imag, right_real, right_imag):
    real_part = contract(left_real, right_real) + contract(left_imag, right_imag)
    imag_part = contract(left_imag, right_real) - contract(left_real, right_imag)
    return (real_part, imag_part)


def rounded(pair):
    return (pair[0].astype(BF16), pair[1].astype(BF16))


def applied(matrix, source, green):
    carried = rounded(product(*matrix, *green))
    grown = product_adjoint(*carried, *matrix)
    return (source[0] + grown[0], source[1] + grown[1])


def phase_table(row_count, column_count, length):
    row_index = jnp.arange(row_count, dtype=jnp.int32)[:, None]
    column_index = jnp.arange(column_count, dtype=jnp.int32)[None, :]
    residue = row_index * column_index % length
    return residue.astype(F32) * (2.0 * math.pi / length)


def finish(spectrum_real, spectrum_imag, weights, energy_count, length):
    forward_scale = energy_count ** (-0.5)
    inverse_scale = length ** (-0.5)
    spectrum_real = spectrum_real * forward_scale
    spectrum_imag = spectrum_imag * forward_scale
    weight_values = weights.astype(F32)
    squared_real = (
        (spectrum_real * spectrum_real - spectrum_imag * spectrum_imag) * weight_values
    ).astype(BF16)
    squared_imag = (2.0 * spectrum_real * spectrum_imag * weight_values).astype(BF16)
    inverse_phase = phase_table(energy_count, length, length)
    inverse_real = jnp.cos(inverse_phase).astype(BF16)
    inverse_imag = jnp.sin(inverse_phase).astype(BF16)
    out_real, out_imag = product(inverse_real, inverse_imag, squared_real, squared_imag)
    return jnp.stack([out_real * inverse_scale, out_imag * inverse_scale], axis=1).astype(BF16)


def local(lesser_in, retarded, coupling, interaction):
    block_order = coupling.shape[-1]
    energy_count = lax.axis_size("energy")
    chips = lax.axis_size("chip")
    length = 2 * energy_count
    second = lax.axis_index("core") == 1
    resolvent = (retarded[0, 0, 0], retarded[0, 0, 1])
    matrix = rounded(product(*resolvent, coupling[0, 0], coupling[0, 1]))
    half = rounded(product(*resolvent, lesser_in[0, 0, 0], lesser_in[0, 0, 1]))
    source = product_adjoint(*half, *resolvent)

    first_source = lax.all_gather(jnp.stack(rounded(source)), "core")[0]
    first_matrix = lax.all_gather(jnp.stack(matrix), "core")[0]
    both_matrix = rounded(product(*matrix, first_matrix[0], first_matrix[1]))
    both_source = applied(matrix, source, (first_source[0], first_source[1]))
    matrix = tuple(jnp.where(second, a, b) for a, b in zip(both_matrix, matrix))
    source = tuple(jnp.where(second, a, b) for a, b in zip(both_source, source))

    incoming = jnp.zeros((2, block_order, block_order), BF16)
    green = jnp.stack(rounded(source))
    for hop in range(chips - 1):
        arrived = lax.ppermute(green, SPACE, [(2 * hop + 1, 2 * hop + 3)])
        incoming = incoming + arrived
        green = jnp.stack(rounded(applied(matrix, source, (incoming[0], incoming[1]))))
    incoming = lax.all_gather(incoming, "core")[1]
    green = jnp.stack(rounded(applied(matrix, source, (incoming[0], incoming[1]))))

    entries = green.reshape(2, energy_count, -1).swapaxes(0, 1)
    entries = lax.all_to_all(entries, "energy", split_axis=0, concat_axis=0, tiled=True)
    forward_phase = phase_table(length, energy_count, length)
    forward_real = jnp.cos(forward_phase).astype(BF16)
    forward_imag = (-jnp.sin(forward_phase)).astype(BF16)
    spectrum_real, spectrum_imag = product(forward_real, forward_imag, entries[:, 0], entries[:, 1])
    result = finish(spectrum_real, spectrum_imag, interaction[0], energy_count, length)
    returned = lax.all_to_all(result, "energy", split_axis=0, concat_axis=0, tiled=True)
    return returned.swapaxes(0, 1).reshape(1, 1, 2, block_order, block_order)


def solution(mesh):
    split = Mesh(
        mesh.devices.reshape(mesh.shape["space"] // 2, 2, mesh.shape["energy"]),
        ("chip", "core", "energy"),
    )
    in_specs = (
        P("energy", SPACE, None, None, None),
        P("energy", SPACE, None, None, None),
        P(SPACE, None, None, None),
        P(SPACE, None, "energy"),
    )
    out_specs = P("energy", SPACE, None, None, None)
    return jax.shard_map(local, mesh=split, in_specs=in_specs, out_specs=out_specs, check_vma=False)
```

```python
import functools
import math

import jax
import jax.numpy as jnp
from jax import lax
from jax.experimental import pallas as pl
from jax.experimental.pallas import tpu as pltpu
from jax.sharding import Mesh
from jax.sharding import PartitionSpec as P

SPACE = ("chip", "core")
BF16 = jnp.bfloat16
F32 = jnp.float32
LANES = 128
ROWS = 8


def dot(left, right):
    return jnp.dot(left, right, preferred_element_type=F32)


def dot_adjoint(left, right):
    return lax.dot_general(left, right, (((1,), (1,)), ((), ())), preferred_element_type=F32)


def product(left, right):
    real_part = dot(left[0], right[0]) - dot(left[1], right[1])
    imag_part = dot(left[0], right[1]) + dot(left[1], right[0])
    return (real_part, imag_part)


def product_adjoint(left, right):
    real_part = dot_adjoint(left[0], right[0]) + dot_adjoint(left[1], right[1])
    imag_part = dot_adjoint(left[1], right[0]) - dot_adjoint(left[0], right[1])
    return (real_part, imag_part)


def rounded(pair):
    return (pair[0].astype(BF16), pair[1].astype(BF16))


def parts(ref):
    return (ref[0], ref[1])


def put(ref, pair):
    ref[0] = pair[0].astype(ref.dtype)
    ref[1] = pair[1].astype(ref.dtype)


def applied(matrix, source, green):
    carried = rounded(product(matrix, green))
    grown = product_adjoint(carried, matrix)
    return (source[0] + grown[0], source[1] + grown[1])


def call(body, outs, *operands, flops=0):
    outs = [jax.ShapeDtypeStruct(shape, dtype) for shape, dtype in outs]
    size = sum(math.prod(a.shape) * a.dtype.itemsize for a in [*operands, *outs])
    return pl.pallas_call(
        body,
        out_shape=outs if len(outs) > 1 else outs[0],
        compiler_params=pltpu.CompilerParams(vmem_limit_bytes=24 * 2**20),
        cost_estimate=pl.CostEstimate(flops=flops, bytes_accessed=size, transcendentals=0),
    )(*operands)


def prelude_body(lesser_ref, retarded_ref, coupling_ref, matrix_ref, source_ref, sent_ref):
    resolvent = parts(retarded_ref)
    half = rounded(product(resolvent, parts(lesser_ref)))
    source = product_adjoint(half, resolvent)
    put(source_ref, source)
    put(sent_ref, source)
    put(matrix_ref, product(resolvent, parts(coupling_ref)))


def pair_source_body(matrix_ref, source_ref, first_ref, out_ref, green_ref):
    @pl.when(lax.axis_index("core") == 1)
    def _():
        total = applied(parts(matrix_ref), parts(source_ref), parts(first_ref.at[0]))
        put(out_ref, total)
        put(green_ref, total)

    @pl.when(lax.axis_index("core") == 0)
    def _():
        put(out_ref, parts(source_ref))
        put(green_ref, parts(source_ref))


def pair_matrix_body(matrix_ref, first_ref, out_ref):
    @pl.when(lax.axis_index("core") == 1)
    def _():
        put(out_ref, product(parts(matrix_ref), parts(first_ref.at[0])))

    @pl.when(lax.axis_index("core") == 0)
    def _():
        put(out_ref, parts(matrix_ref))


def hop_body(matrix_ref, source_ref, incoming_ref, green_ref):
    put(green_ref, applied(parts(matrix_ref), parts(source_ref), parts(incoming_ref)))


def lower(shape):
    return lax.broadcasted_iota(jnp.int32, shape, 1) < ROWS // 2


def chunked(part):
    left = part[:, :LANES].reshape(-1, ROWS, LANES)
    right = part[:, LANES:].reshape(-1, ROWS, LANES)
    first = lower(left.shape)
    even = jnp.where(first, left, pltpu.roll(right, ROWS // 2, 1))
    odd = jnp.where(first, pltpu.roll(left, ROWS // 2, 1), right)
    return even, odd


def unchunked(even, odd):
    first = lower(even.shape)
    left = jnp.where(first, even, pltpu.roll(odd, ROWS // 2, 1))
    right = jnp.where(first, pltpu.roll(even, ROWS // 2, 1), odd)
    return left.reshape(-1, LANES), right.reshape(-1, LANES)


def last_body(matrix_ref, source_ref, incoming_ref, out_ref):
    green = applied(parts(matrix_ref), parts(source_ref), parts(incoming_ref.at[1]))
    even_real, odd_real = chunked(green[0])
    even_imag, odd_imag = chunked(green[1])
    out_ref[:, 0] = jnp.concatenate([even_real, even_imag], axis=1).astype(BF16)
    out_ref[:, 1] = jnp.concatenate([odd_real, odd_imag], axis=1).astype(BF16)


def spectra_body(chunks_ref, forward_ref, inverse_ref, weights_ref, out_ref, rows_ref):
    count = chunks_ref.shape[0]
    length = weights_ref.shape[0]
    stride = 2 * ROWS
    rows_ref[...] = chunks_ref[...].astype(F32).reshape(rows_ref.shape)
    taken = [rows_ref[pl.ds(i, count, stride=stride), :].astype(BF16) for i in range(stride)]
    values = jnp.concatenate(
        [jnp.concatenate(taken[:ROWS], axis=1), jnp.concatenate(taken[ROWS:], axis=1)], axis=0
    )
    spectrum = dot(forward_ref[...], values) * (count**-0.5)
    order = [2 * (i % 4) + i // 4 for i in range(ROWS)]
    weights = jnp.concatenate(
        [weights_ref[:, LANES * i : LANES * (i + 1)] for i in order], axis=1
    ).astype(F32)
    real, imag = spectrum[:length], spectrum[length:]
    squared_real = ((real * real - imag * imag) * weights).astype(BF16)
    squared_imag = (2.0 * real * imag * weights).astype(BF16)
    result = dot(inverse_ref[...], jnp.concatenate([squared_real, squared_imag], axis=0))
    result = result * (length**-0.5)
    for i in range(ROWS):
        columns = slice(LANES * i, LANES * (i + 1))
        rows_ref[pl.ds(i, count, stride=stride), :] = result[:count, columns]
        rows_ref[pl.ds(i + ROWS, count, stride=stride), :] = result[count:, columns]
    out_ref[...] = rows_ref[...].reshape(out_ref.shape).astype(BF16)


def output_body(chunks_ref, out_ref):
    even = chunks_ref[:, 0].astype(F32)
    odd = chunks_ref[:, 1].astype(F32)
    for part in range(2):
        rows = slice(ROWS * part, ROWS * (part + 1))
        left, right = unchunked(even[:, rows], odd[:, rows])
        out_ref[part] = jnp.concatenate([left, right], axis=1).astype(BF16)


def phase_table(row_count, column_count, length):
    row_index = jnp.arange(row_count, dtype=jnp.int32)[:, None]
    column_index = jnp.arange(column_count, dtype=jnp.int32)[None, :]
    residue = row_index * column_index % length
    return residue.astype(F32) * (2.0 * math.pi / length)


def complex_table(real, imag):
    return jnp.block([[real, -imag], [imag, real]]).astype(BF16)


def spectra(chunks, weights):
    count = chunks.shape[0]
    length = weights.shape[0]
    phase = phase_table(length, count, length)
    forward = complex_table(jnp.cos(phase), -jnp.sin(phase))
    phase = phase_table(count, length, length)
    inverse = complex_table(jnp.cos(phase), jnp.sin(phase))
    return pl.pallas_call(
        spectra_body,
        out_shape=jax.ShapeDtypeStruct(chunks.shape, BF16),
        scratch_shapes=[pltpu.VMEM((count * 2 * ROWS, LANES), F32)],
        compiler_params=pltpu.CompilerParams(vmem_limit_bytes=24 * 2**20),
        cost_estimate=pl.CostEstimate(
            flops=16 * length * count * LANES * ROWS, bytes_accessed=3 * 2**18, transcendentals=0
        ),
    )(chunks, forward, inverse, weights)


def local(lesser_in, retarded, coupling, interaction):
    order = coupling.shape[-1]
    chips = lax.axis_size("chip")
    energies = lax.axis_size("energy")
    shape = (2, order, order)
    chunk = (energies, 2 * ROWS, LANES)
    one = 8 * order**3

    matrix, source, sent = call(
        prelude_body,
        [(shape, BF16), (shape, F32), (shape, BF16)],
        lesser_in[0, 0],
        retarded[0, 0],
        coupling[0],
        flops=3 * one,
    )
    first_source = lax.all_gather(sent, "core")
    source, green = call(
        pair_source_body,
        [(shape, F32), (shape, BF16)],
        matrix,
        source,
        first_source,
        flops=2 * one,
    )
    first_matrix = lax.all_gather(matrix, "core")
    matrix = call(pair_matrix_body, [(shape, BF16)], matrix, first_matrix, flops=one)
    incoming = None
    for hop in range(chips - 1):
        arrived = lax.ppermute(green, SPACE, [(2 * hop + 1, 2 * hop + 3)])
        incoming = arrived if incoming is None else incoming + arrived
        if hop < chips - 2:
            green = call(hop_body, [(shape, BF16)], matrix, source, incoming, flops=2 * one)
    incoming = lax.all_gather(incoming, "core")
    chunks = call(
        last_body,
        [((energies // 2, 2, 2 * ROWS, LANES), BF16)],
        matrix,
        source,
        incoming,
        flops=2 * one,
    )
    chunks = lax.all_to_all(
        chunks.reshape(chunk), "energy", split_axis=0, concat_axis=0, tiled=True
    )
    result = spectra(chunks, interaction[0])
    returned = lax.all_to_all(result, "energy", split_axis=0, concat_axis=0, tiled=True)
    out = call(
        output_body,
        [(shape, BF16)],
        returned.reshape(energies // 2, 2, 2 * ROWS, LANES),
    )
    return out.reshape(1, 1, *shape)


def solution(mesh):
    split = Mesh(
        mesh.devices.reshape(mesh.shape["space"] // 2, 2, mesh.shape["energy"]),
        ("chip", "core", "energy"),
    )
    in_specs = (
        P("energy", SPACE, None, None, None),
        P("energy", SPACE, None, None, None),
        P(SPACE, None, None, None),
        P(SPACE, None, "energy"),
    )
    out_specs = P("energy", SPACE, None, None, None)
    return jax.shard_map(local, mesh=split, in_specs=in_specs, out_specs=out_specs, check_vma=False)
```

```python
import functools
import math

import jax
import jax.numpy as jnp
from jax import lax
from jax.experimental import pallas as pl
from jax.experimental.pallas import tpu as pltpu
from jax.sharding import Mesh
from jax.sharding import PartitionSpec as P

SPACE = ("chip", "core")
BF16 = jnp.bfloat16
F32 = jnp.float32
LANES = 128
ROWS = 8
FIRST_OUT = 42
FIRST_BACK = 42


def dot(left, right):
    return jnp.dot(left, right, preferred_element_type=F32)


def dot_adjoint(left, right):
    return lax.dot_general(left, right, (((1,), (1,)), ((), ())), preferred_element_type=F32)


def product(left, right):
    real_part = dot(left[0], right[0]) - dot(left[1], right[1])
    imag_part = dot(left[0], right[1]) + dot(left[1], right[0])
    return (real_part, imag_part)


def product_adjoint(left, right):
    real_part = dot_adjoint(left[0], right[0]) + dot_adjoint(left[1], right[1])
    imag_part = dot_adjoint(left[1], right[0]) - dot_adjoint(left[0], right[1])
    return (real_part, imag_part)


def rounded(pair):
    return (pair[0].astype(BF16), pair[1].astype(BF16))


def parts(ref):
    return (ref[0], ref[1])


def put(ref, pair):
    ref[0] = pair[0].astype(ref.dtype)
    ref[1] = pair[1].astype(ref.dtype)


def applied(matrix, source, green):
    carried = rounded(product(matrix, green))
    grown = product_adjoint(carried, matrix)
    return (source[0] + grown[0], source[1] + grown[1])


def call(body, outs, *operands, flops=0):
    outs = [jax.ShapeDtypeStruct(shape, dtype) for shape, dtype in outs]
    size = sum(math.prod(a.shape) * a.dtype.itemsize for a in [*operands, *outs])
    return pl.pallas_call(
        body,
        out_shape=outs if len(outs) > 1 else outs[0],
        compiler_params=pltpu.CompilerParams(vmem_limit_bytes=24 * 2**20),
        cost_estimate=pl.CostEstimate(flops=flops, bytes_accessed=size, transcendentals=0),
    )(*operands)


def prelude_body(
    lesser_hbm, retarded_hbm, coupling_hbm, matrix_ref, source_ref, sent_ref, loaded, semaphores
):
    copies = [
        pltpu.make_async_copy(ref, loaded.at[i], semaphores.at[i])
        for i, ref in enumerate((retarded_hbm, lesser_hbm, coupling_hbm))
    ]
    for copy in copies:
        copy.start()
    copies[0].wait()
    copies[1].wait()
    resolvent = parts(loaded.at[0])
    half = rounded(product(resolvent, parts(loaded.at[1])))
    source = product_adjoint(half, resolvent)
    put(source_ref, source)
    put(sent_ref, source)
    copies[2].wait()
    put(matrix_ref, product(resolvent, parts(loaded.at[2])))


def prelude(lesser_in, retarded, coupling):
    shape = coupling.shape
    return pl.pallas_call(
        prelude_body,
        out_shape=[jax.ShapeDtypeStruct(shape, dtype) for dtype in (BF16, F32, BF16)],
        in_specs=[pl.BlockSpec(memory_space=pltpu.HBM)] * 3,
        out_specs=[pl.BlockSpec(memory_space=pltpu.VMEM)] * 3,
        scratch_shapes=[pltpu.VMEM((3, *shape), BF16), pltpu.SemaphoreType.DMA((3,))],
        compiler_params=pltpu.CompilerParams(vmem_limit_bytes=24 * 2**20),
        cost_estimate=pl.CostEstimate(
            flops=24 * shape[-1] ** 3, bytes_accessed=2**20, transcendentals=0
        ),
    )(*(pltpu.with_memory_space_constraint(a, pltpu.HBM) for a in (lesser_in, retarded, coupling)))


def pair_source_body(matrix_ref, source_ref, first_ref, out_ref, green_ref):
    @pl.when(lax.axis_index("core") == 1)
    def _():
        total = applied(parts(matrix_ref), parts(source_ref), parts(first_ref.at[0]))
        put(out_ref, total)
        put(green_ref, total)

    @pl.when(lax.axis_index("core") == 0)
    def _():
        put(out_ref, parts(source_ref))
        put(green_ref, parts(source_ref))


def pair_matrix_body(matrix_ref, first_ref, out_ref):
    @pl.when(lax.axis_index("core") == 1)
    def _():
        put(out_ref, product(parts(matrix_ref), parts(first_ref.at[0])))

    @pl.when(lax.axis_index("core") == 0)
    def _():
        put(out_ref, parts(matrix_ref))


def hop_body(matrix_ref, source_ref, incoming_ref, green_ref):
    put(green_ref, applied(parts(matrix_ref), parts(source_ref), parts(incoming_ref)))


def joined_body(source_ref, matrix_ref, near_ref, far_ref, out_ref):
    @pl.when(lax.axis_index("chip") == 3)
    def _():
        put(out_ref, applied(parts(matrix_ref), parts(source_ref), parts(far_ref)))

    @pl.when(lax.axis_index("chip") != 3)
    def _():
        out_ref[...] = source_ref[...] + near_ref[...]


def lower(shape):
    return lax.broadcasted_iota(jnp.int32, shape, 1) < ROWS // 2


def chunked(part):
    left = part[:, :LANES].reshape(-1, ROWS, LANES)
    right = part[:, LANES:].reshape(-1, ROWS, LANES)
    first = lower(left.shape)
    even = jnp.where(first, left, pltpu.roll(right, ROWS // 2, 1))
    odd = jnp.where(first, pltpu.roll(left, ROWS // 2, 1), right)
    return even, odd


def unchunked(even, odd):
    first = lower(even.shape)
    left = jnp.where(first, even, pltpu.roll(odd, ROWS // 2, 1))
    right = jnp.where(first, pltpu.roll(even, ROWS // 2, 1), odd)
    return left.reshape(-1, LANES), right.reshape(-1, LANES)


def rolled(count, start):
    if start == 0:
        return [(slice(0, count), slice(0, count))]
    return [
        (slice(0, count - start), slice(start, count)),
        (slice(count - start, count), slice(0, start)),
    ]


def last_body(matrix_ref, source_ref, incoming_ref, out_ref):
    green = applied(parts(matrix_ref), parts(source_ref), parts(incoming_ref.at[1]))
    even_real, odd_real = chunked(green[0])
    even_imag, odd_imag = chunked(green[1])
    even = jnp.concatenate([even_real, even_imag], axis=1).astype(BF16)
    odd = jnp.concatenate([odd_real, odd_imag], axis=1).astype(BF16)
    pairs = out_ref.shape[0]
    start = FIRST_OUT // 2
    for target, taken in rolled(pairs, start):
        out_ref[target, 0] = even[taken]
        out_ref[target, 1] = odd[taken]


def spectra_body(chunks_ref, forward_ref, inverse_ref, weights_ref, out_ref, rows_ref):
    count = chunks_ref.shape[0]
    length = weights_ref.shape[0]
    stride = 2 * ROWS
    rows_ref[...] = chunks_ref[...].astype(F32).reshape(rows_ref.shape)
    taken = [rows_ref[pl.ds(i, count, stride=stride), :].astype(BF16) for i in range(stride)]
    values = jnp.concatenate(
        [jnp.concatenate(taken[:ROWS], axis=1), jnp.concatenate(taken[ROWS:], axis=1)], axis=0
    )
    spectrum = dot(forward_ref[...], values) * (count**-0.5)
    order = [2 * (i % 4) + i // 4 for i in range(ROWS)]
    weights = jnp.concatenate(
        [weights_ref[:, LANES * i : LANES * (i + 1)] for i in order], axis=1
    ).astype(F32)
    real, imag = spectrum[:length], spectrum[length:]
    squared_real = ((real * real - imag * imag) * weights).astype(BF16)
    squared_imag = (2.0 * real * imag * weights).astype(BF16)
    result = dot(inverse_ref[...], jnp.concatenate([squared_real, squared_imag], axis=0))
    result = result * (length**-0.5)
    for i in range(ROWS):
        columns = slice(LANES * i, LANES * (i + 1))
        rows_ref[pl.ds(i, count, stride=stride), :] = result[:count, columns]
        rows_ref[pl.ds(i + ROWS, count, stride=stride), :] = result[count:, columns]
    out_ref[...] = rows_ref[...].reshape(out_ref.shape).astype(BF16)


def output_body(chunks_ref, out_ref):
    even = chunks_ref[:, 0].astype(F32)
    odd = chunks_ref[:, 1].astype(F32)
    for part in range(2):
        rows = slice(ROWS * part, ROWS * (part + 1))
        left, right = unchunked(even[:, rows], odd[:, rows])
        value = jnp.concatenate([left, right], axis=1).astype(BF16)
        for taken, target in rolled(value.shape[0], 2 * ROWS // 4 * FIRST_BACK):
            out_ref[part, target] = value[taken]


def phase_table(row_count, column_count, length):
    row_index = jnp.arange(row_count, dtype=jnp.int32)[:, None]
    column_index = jnp.arange(column_count, dtype=jnp.int32)[None, :]
    residue = row_index * column_index % length
    return residue.astype(F32) * (2.0 * math.pi / length)


def complex_table(real, imag):
    return jnp.block([[real, -imag], [imag, real]]).astype(BF16)


def spectra(chunks, weights):
    count = chunks.shape[0]
    length = weights.shape[0]
    phase = phase_table(length, count, length)
    phase = jnp.roll(phase, -FIRST_OUT, axis=1)
    forward = complex_table(jnp.cos(phase), -jnp.sin(phase))
    phase = phase_table(count, length, length)
    phase = jnp.roll(phase, -FIRST_BACK, axis=0)
    inverse = complex_table(jnp.cos(phase), jnp.sin(phase))
    return pl.pallas_call(
        spectra_body,
        out_shape=jax.ShapeDtypeStruct(chunks.shape, BF16),
        scratch_shapes=[pltpu.VMEM((count * 2 * ROWS, LANES), F32)],
        compiler_params=pltpu.CompilerParams(vmem_limit_bytes=24 * 2**20),
        cost_estimate=pl.CostEstimate(
            flops=16 * length * count * LANES * ROWS, bytes_accessed=3 * 2**18, transcendentals=0
        ),
    )(chunks, forward, inverse, weights)


def exchanged(chunks, first):
    count = chunks.shape[0]
    group = [(first + i) % count for i in range(count)]
    return lax.all_to_all(
        chunks, "energy", split_axis=0, concat_axis=0, axis_index_groups=[group], tiled=True
    )


def local(lesser_in, retarded, coupling, interaction):
    order = coupling.shape[-1]
    energies = lax.axis_size("energy")
    shape = (2, order, order)
    chunk = (energies, 2 * ROWS, LANES)
    one = 8 * order**3

    matrix, source, sent = prelude(lesser_in[0, 0], retarded[0, 0], coupling[0])
    first_source = lax.all_gather(sent, "core")
    source, green = call(
        pair_source_body,
        [(shape, F32), (shape, BF16)],
        matrix,
        source,
        first_source,
        flops=2 * one,
    )
    first_matrix = lax.all_gather(matrix, "core")
    matrix = call(pair_matrix_body, [(shape, BF16)], matrix, first_matrix, flops=one)
    arrived_source = lax.ppermute(green, SPACE, [(1, 3), (5, 7)])
    arrived_matrix = lax.ppermute(matrix, SPACE, [(5, 7)])
    green = call(hop_body, [(shape, BF16)], matrix, source, arrived_source, flops=2 * one)
    far = lax.ppermute(green, SPACE, [(3, 7)])
    near = lax.ppermute(green, SPACE, [(3, 5)])
    incoming = call(
        joined_body, [(shape, BF16)], arrived_source, arrived_matrix, near, far, flops=2 * one
    )
    incoming = lax.all_gather(incoming, "core")
    chunks = call(
        last_body,
        [((energies // 2, 2, 2 * ROWS, LANES), BF16)],
        matrix,
        source,
        incoming,
        flops=2 * one,
    )
    chunks = exchanged(chunks.reshape(chunk), FIRST_OUT)
    result = spectra(chunks, interaction[0])
    returned = exchanged(result, FIRST_BACK)
    out = call(
        output_body,
        [(shape, BF16)],
        returned.reshape(energies // 2, 2, 2 * ROWS, LANES),
    )
    return out.reshape(1, 1, *shape)


def solution(mesh):
    split = Mesh(
        mesh.devices.reshape(mesh.shape["space"] // 2, 2, mesh.shape["energy"]),
        ("chip", "core", "energy"),
    )
    in_specs = (
        P("energy", SPACE, None, None, None),
        P("energy", SPACE, None, None, None),
        P(SPACE, None, None, None),
        P(SPACE, None, "energy"),
    )
    out_specs = P("energy", SPACE, None, None, None)
    return jax.shard_map(local, mesh=split, in_specs=in_specs, out_specs=out_specs, check_vma=False)
```

```python
import functools
import math

import jax
import jax.numpy as jnp
from jax import lax
from jax.experimental import pallas as pl
from jax.experimental.pallas import tpu as pltpu
from jax.sharding import Mesh
from jax.sharding import PartitionSpec as P

SPACE = ("chip", "core")
BF16 = jnp.bfloat16
F32 = jnp.float32
LANES = 128
ROWS = 8
FIRST_OUT = 42
FIRST_BACK = 42


def dot(left, right):
    return jnp.dot(left, right, preferred_element_type=F32)


def dot_adjoint(left, right):
    return lax.dot_general(left, right, (((1,), (1,)), ((), ())), preferred_element_type=F32)


def product(left, right):
    real_part = dot(left[0], right[0]) - dot(left[1], right[1])
    imag_part = dot(left[0], right[1]) + dot(left[1], right[0])
    return (real_part, imag_part)


def product_adjoint(left, right):
    real_part = dot_adjoint(left[0], right[0]) + dot_adjoint(left[1], right[1])
    imag_part = dot_adjoint(left[1], right[0]) - dot_adjoint(left[0], right[1])
    return (real_part, imag_part)


def rounded(pair):
    return (pair[0].astype(BF16), pair[1].astype(BF16))


def parts(ref):
    return (ref[0], ref[1])


def put(ref, pair):
    ref[0] = pair[0].astype(ref.dtype)
    ref[1] = pair[1].astype(ref.dtype)


def applied(matrix, source, green):
    carried = rounded(product(matrix, green))
    grown = product_adjoint(carried, matrix)
    return (source[0] + grown[0], source[1] + grown[1])


def call(body, outs, *operands, flops=0):
    outs = [jax.ShapeDtypeStruct(shape, dtype) for shape, dtype in outs]
    size = sum(math.prod(a.shape) * a.dtype.itemsize for a in [*operands, *outs])
    return pl.pallas_call(
        body,
        out_shape=outs if len(outs) > 1 else outs[0],
        compiler_params=pltpu.CompilerParams(vmem_limit_bytes=24 * 2**20),
        cost_estimate=pl.CostEstimate(flops=flops, bytes_accessed=size, transcendentals=0),
    )(*operands)


def prelude_body(
    lesser_hbm, retarded_hbm, coupling_hbm, matrix_ref, source_ref, sent_ref, loaded, semaphores
):
    copies = [
        pltpu.make_async_copy(ref, loaded.at[i], semaphores.at[i])
        for i, ref in enumerate((retarded_hbm, lesser_hbm, coupling_hbm))
    ]
    for copy in copies:
        copy.start()
    copies[0].wait()
    copies[1].wait()
    resolvent = parts(loaded.at[0])
    half = rounded(product(resolvent, parts(loaded.at[1])))
    source = product_adjoint(half, resolvent)
    put(source_ref, source)
    put(sent_ref, source)
    copies[2].wait()
    put(matrix_ref, product(resolvent, parts(loaded.at[2])))


def prelude(lesser_in, retarded, coupling):
    shape = coupling.shape
    return pl.pallas_call(
        prelude_body,
        out_shape=[jax.ShapeDtypeStruct(shape, dtype) for dtype in (BF16, F32, BF16)],
        in_specs=[pl.BlockSpec(memory_space=pltpu.HBM)] * 3,
        out_specs=[pl.BlockSpec(memory_space=pltpu.VMEM)] * 3,
        scratch_shapes=[pltpu.VMEM((3, *shape), BF16), pltpu.SemaphoreType.DMA((3,))],
        compiler_params=pltpu.CompilerParams(vmem_limit_bytes=24 * 2**20),
        cost_estimate=pl.CostEstimate(
            flops=24 * shape[-1] ** 3, bytes_accessed=2**20, transcendentals=0
        ),
    )(*(pltpu.with_memory_space_constraint(a, pltpu.HBM) for a in (lesser_in, retarded, coupling)))


def is_at(**place):
    tests = [lax.axis_index(axis) == index for axis, index in place.items()]
    return functools.reduce(jnp.logical_and, tests)


def leading_body(matrix_ref, source_ref, first_ref, green_ref):
    @pl.when(is_at(chip=0, core=1))
    def _():
        put(green_ref, applied(parts(matrix_ref), parts(source_ref), parts(first_ref.at[0])))


def pair_body(
    matrix_ref, source_ref, first_source_ref, first_matrix_ref, out_ref, total_ref, sent_ref
):
    @pl.when(is_at(core=1))
    def _():
        matrix = parts(matrix_ref)
        total = applied(matrix, parts(source_ref), parts(first_source_ref.at[0]))
        put(total_ref, total)
        put(sent_ref.at[0], total)
        both = product(matrix, parts(first_matrix_ref.at[0]))
        put(out_ref, both)
        put(sent_ref.at[1], both)

    @pl.when(is_at(core=0))
    def _():
        put(out_ref, parts(matrix_ref))
        put(total_ref, parts(source_ref))


def hop_body(matrix_ref, source_ref, incoming_ref, green_ref):
    @pl.when(is_at(chip=1, core=1))
    def _():
        put(green_ref, applied(parts(matrix_ref), parts(source_ref), parts(incoming_ref)))


def joined_body(arrived_ref, map_ref, far_ref, near_ref, out_ref):
    @pl.when(is_at(chip=3, core=1))
    def _():
        put(out_ref, applied(parts(map_ref.at[1]), parts(map_ref.at[0]), parts(far_ref)))

    @pl.when(jnp.logical_not(is_at(chip=3, core=1)))
    def _():
        out_ref[...] = arrived_ref[...] + near_ref[...]


def lower(shape):
    return lax.broadcasted_iota(jnp.int32, shape, 1) < ROWS // 2


def chunked(part):
    left = part[:, :LANES].reshape(-1, ROWS, LANES)
    right = part[:, LANES:].reshape(-1, ROWS, LANES)
    first = lower(left.shape)
    even = jnp.where(first, left, pltpu.roll(right, ROWS // 2, 1))
    odd = jnp.where(first, pltpu.roll(left, ROWS // 2, 1), right)
    return even, odd


def unchunked(even, odd):
    first = lower(even.shape)
    left = jnp.where(first, even, pltpu.roll(odd, ROWS // 2, 1))
    right = jnp.where(first, pltpu.roll(even, ROWS // 2, 1), odd)
    return left.reshape(-1, LANES), right.reshape(-1, LANES)


def rolled(count, start):
    if start == 0:
        return [(slice(0, count), slice(0, count))]
    return [
        (slice(0, count - start), slice(start, count)),
        (slice(count - start, count), slice(0, start)),
    ]


def last_body(matrix_ref, source_ref, incoming_ref, out_ref):
    green = applied(parts(matrix_ref), parts(source_ref), parts(incoming_ref.at[1]))
    even_real, odd_real = chunked(green[0])
    even_imag, odd_imag = chunked(green[1])
    even = jnp.concatenate([even_real, even_imag], axis=1).astype(BF16)
    odd = jnp.concatenate([odd_real, odd_imag], axis=1).astype(BF16)
    pairs = out_ref.shape[0]
    start = FIRST_OUT // 2
    for target, taken in rolled(pairs, start):
        out_ref[target, 0] = even[taken]
        out_ref[target, 1] = odd[taken]


def spectra_body(chunks_ref, forward_ref, inverse_ref, weights_ref, out_ref, rows_ref):
    count = chunks_ref.shape[0]
    length = weights_ref.shape[0]
    stride = 2 * ROWS
    rows_ref[...] = chunks_ref[...].astype(F32).reshape(rows_ref.shape)
    taken = [rows_ref[pl.ds(i, count, stride=stride), :].astype(BF16) for i in range(stride)]
    values = jnp.concatenate(
        [jnp.concatenate(taken[:ROWS], axis=1), jnp.concatenate(taken[ROWS:], axis=1)], axis=0
    )
    spectrum = dot(forward_ref[...], values) * (count**-0.5)
    order = [2 * (i % 4) + i // 4 for i in range(ROWS)]
    weights = jnp.concatenate(
        [weights_ref[:, LANES * i : LANES * (i + 1)] for i in order], axis=1
    ).astype(F32)
    real, imag = spectrum[:length], spectrum[length:]
    squared_real = ((real * real - imag * imag) * weights).astype(BF16)
    squared_imag = (2.0 * real * imag * weights).astype(BF16)
    result = dot(inverse_ref[...], jnp.concatenate([squared_real, squared_imag], axis=0))
    result = result * (length**-0.5)
    for i in range(ROWS):
        columns = slice(LANES * i, LANES * (i + 1))
        rows_ref[pl.ds(i, count, stride=stride), :] = result[:count, columns]
        rows_ref[pl.ds(i + ROWS, count, stride=stride), :] = result[count:, columns]
    out_ref[...] = rows_ref[...].reshape(out_ref.shape).astype(BF16)


def output_body(chunks_ref, out_ref):
    even = chunks_ref[:, 0].astype(F32)
    odd = chunks_ref[:, 1].astype(F32)
    for part in range(2):
        rows = slice(ROWS * part, ROWS * (part + 1))
        left, right = unchunked(even[:, rows], odd[:, rows])
        value = jnp.concatenate([left, right], axis=1).astype(BF16)
        for taken, target in rolled(value.shape[0], 2 * ROWS // 4 * FIRST_BACK):
            out_ref[part, target] = value[taken]


def phase_table(row_count, column_count, length):
    row_index = jnp.arange(row_count, dtype=jnp.int32)[:, None]
    column_index = jnp.arange(column_count, dtype=jnp.int32)[None, :]
    residue = row_index * column_index % length
    return residue.astype(F32) * (2.0 * math.pi / length)


def complex_table(real, imag):
    return jnp.block([[real, -imag], [imag, real]]).astype(BF16)


def spectra(chunks, weights):
    count = chunks.shape[0]
    length = weights.shape[0]
    phase = phase_table(length, count, length)
    phase = jnp.roll(phase, -FIRST_OUT, axis=1)
    forward = complex_table(jnp.cos(phase), -jnp.sin(phase))
    phase = phase_table(count, length, length)
    phase = jnp.roll(phase, -FIRST_BACK, axis=0)
    inverse = complex_table(jnp.cos(phase), jnp.sin(phase))
    return pl.pallas_call(
        spectra_body,
        out_shape=jax.ShapeDtypeStruct(chunks.shape, BF16),
        scratch_shapes=[pltpu.VMEM((count * 2 * ROWS, LANES), F32)],
        compiler_params=pltpu.CompilerParams(vmem_limit_bytes=24 * 2**20),
        cost_estimate=pl.CostEstimate(
            flops=16 * length * count * LANES * ROWS, bytes_accessed=3 * 2**18, transcendentals=0
        ),
    )(chunks, forward, inverse, weights)


def exchanged(chunks, first):
    count = chunks.shape[0]
    group = [(first + i) % count for i in range(count)]
    return lax.all_to_all(
        chunks, "energy", split_axis=0, concat_axis=0, axis_index_groups=[group], tiled=True
    )


def local(lesser_in, retarded, coupling, interaction):
    order = coupling.shape[-1]
    energies = lax.axis_size("energy")
    shape = (2, order, order)
    chunk = (energies, 2 * ROWS, LANES)
    one = 8 * order**3

    matrix, source, sent = prelude(lesser_in[0, 0], retarded[0, 0], coupling[0])
    first_source = lax.all_gather(sent, "core")
    green = call(leading_body, [(shape, BF16)], matrix, source, first_source, flops=2 * one)
    arrived = lax.ppermute(green, SPACE, [(1, 3)])
    first_matrix = lax.all_gather(matrix, "core")
    matrix, source, sent = call(
        pair_body,
        [(shape, BF16), (shape, F32), ((2, *shape), BF16)],
        matrix,
        source,
        first_source,
        first_matrix,
        flops=3 * one,
    )
    chip_map = lax.ppermute(sent, SPACE, [(5, 7)])
    green = call(hop_body, [(shape, BF16)], matrix, source, arrived, flops=2 * one)
    near = lax.ppermute(green, SPACE, [(3, 5)])
    far = lax.ppermute(green, SPACE, [(3, 7)])
    incoming = call(joined_body, [(shape, BF16)], arrived, chip_map, far, near, flops=2 * one)
    incoming = lax.all_gather(incoming, "core")
    chunks = call(
        last_body,
        [((energies // 2, 2, 2 * ROWS, LANES), BF16)],
        matrix,
        source,
        incoming,
        flops=2 * one,
    )
    chunks = exchanged(chunks.reshape(chunk), FIRST_OUT)
    result = spectra(chunks, interaction[0])
    returned = exchanged(result, FIRST_BACK)
    out = call(
        output_body,
        [(shape, BF16)],
        returned.reshape(energies // 2, 2, 2 * ROWS, LANES),
    )
    return out.reshape(1, 1, *shape)


def solution(mesh):
    split = Mesh(
        mesh.devices.reshape(mesh.shape["space"] // 2, 2, mesh.shape["energy"]),
        ("chip", "core", "energy"),
    )
    in_specs = (
        P("energy", SPACE, None, None, None),
        P("energy", SPACE, None, None, None),
        P(SPACE, None, None, None),
        P(SPACE, None, "energy"),
    )
    out_specs = P("energy", SPACE, None, None, None)
    return jax.shard_map(local, mesh=split, in_specs=in_specs, out_specs=out_specs, check_vma=False)
```

```python
import functools
import math

import jax
import jax.numpy as jnp
import ml_dtypes
import numpy as np
from jax import lax
from jax.experimental import pallas as pl
from jax.experimental.pallas import tpu as pltpu
from jax.sharding import Mesh
from jax.sharding import PartitionSpec as P

SPACE = ("chip", "core")
BF16 = jnp.bfloat16
F32 = jnp.float32
LANES = 128
ROWS = 8
FIRST_OUT = 42
FIRST_BACK = 42


def dot(left, right):
    return jnp.dot(left, right, preferred_element_type=F32)


def dot_adjoint(left, right):
    return lax.dot_general(left, right, (((1,), (1,)), ((), ())), preferred_element_type=F32)


def product(left, right):
    real_part = dot(left[0], right[0]) - dot(left[1], right[1])
    imag_part = dot(left[0], right[1]) + dot(left[1], right[0])
    return (real_part, imag_part)


def product_adjoint(left, right):
    real_part = dot_adjoint(left[0], right[0]) + dot_adjoint(left[1], right[1])
    imag_part = dot_adjoint(left[1], right[0]) - dot_adjoint(left[0], right[1])
    return (real_part, imag_part)


def rounded(pair):
    return (pair[0].astype(BF16), pair[1].astype(BF16))


def parts(ref):
    return (ref[0], ref[1])


def put(ref, pair):
    ref[0] = pair[0].astype(ref.dtype)
    ref[1] = pair[1].astype(ref.dtype)


def applied(matrix, source, green):
    carried = rounded(product(matrix, green))
    grown = product_adjoint(carried, matrix)
    return (source[0] + grown[0], source[1] + grown[1])


def call(body, outs, *operands, flops=0):
    outs = [jax.ShapeDtypeStruct(shape, dtype) for shape, dtype in outs]
    size = sum(math.prod(a.shape) * a.dtype.itemsize for a in [*operands, *outs])
    return pl.pallas_call(
        body,
        out_shape=outs if len(outs) > 1 else outs[0],
        compiler_params=pltpu.CompilerParams(vmem_limit_bytes=24 * 2**20),
        cost_estimate=pl.CostEstimate(flops=flops, bytes_accessed=size, transcendentals=0),
    )(*operands)


def prelude_body(
    lesser_hbm, retarded_hbm, coupling_hbm, matrix_ref, source_ref, sent_ref, loaded, semaphores
):
    copies = [
        pltpu.make_async_copy(ref, loaded.at[i], semaphores.at[i])
        for i, ref in enumerate((retarded_hbm, lesser_hbm, coupling_hbm))
    ]
    for copy in copies:
        copy.start()
    copies[0].wait()
    copies[1].wait()
    resolvent = parts(loaded.at[0])
    half = rounded(product(resolvent, parts(loaded.at[1])))
    source = product_adjoint(half, resolvent)
    put(source_ref, source)
    put(sent_ref, source)
    copies[2].wait()
    put(matrix_ref, product(resolvent, parts(loaded.at[2])))


def prelude(lesser_in, retarded, coupling):
    shape = coupling.shape
    return pl.pallas_call(
        prelude_body,
        out_shape=[jax.ShapeDtypeStruct(shape, dtype) for dtype in (BF16, F32, BF16)],
        in_specs=[pl.BlockSpec(memory_space=pltpu.HBM)] * 3,
        out_specs=[pl.BlockSpec(memory_space=pltpu.VMEM)] * 3,
        scratch_shapes=[pltpu.VMEM((3, *shape), BF16), pltpu.SemaphoreType.DMA((3,))],
        compiler_params=pltpu.CompilerParams(vmem_limit_bytes=24 * 2**20),
        cost_estimate=pl.CostEstimate(
            flops=24 * shape[-1] ** 3, bytes_accessed=2**20, transcendentals=0
        ),
    )(*(pltpu.with_memory_space_constraint(a, pltpu.HBM) for a in (lesser_in, retarded, coupling)))


def is_at(**place):
    tests = [lax.axis_index(axis) == index for axis, index in place.items()]
    return functools.reduce(jnp.logical_and, tests)


def leading_body(matrix_ref, source_ref, first_ref, green_ref):
    @pl.when(is_at(chip=0, core=1))
    def _():
        put(green_ref, applied(parts(matrix_ref), parts(source_ref), parts(first_ref.at[0])))


def pair_body(
    matrix_ref,
    source_ref,
    first_source_ref,
    first_matrix_ref,
    weights_hbm,
    forward_hbm,
    inverse_hbm,
    out_ref,
    total_ref,
    sent_ref,
    weights_ref,
    forward_ref,
    inverse_ref,
    semaphores,
):
    pairs = ((weights_hbm, weights_ref), (forward_hbm, forward_ref), (inverse_hbm, inverse_ref))
    copies = [pltpu.make_async_copy(*pair, semaphores.at[i]) for i, pair in enumerate(pairs)]
    for copy in copies:
        copy.start()

    @pl.when(is_at(core=1))
    def _():
        matrix = parts(matrix_ref)
        total = applied(matrix, parts(source_ref), parts(first_source_ref.at[0]))
        put(total_ref, total)
        put(sent_ref.at[0], total)
        both = product(matrix, parts(first_matrix_ref.at[0]))
        put(out_ref, both)
        put(sent_ref.at[1], both)

    @pl.when(is_at(core=0))
    def _():
        put(out_ref, parts(matrix_ref))
        put(total_ref, parts(source_ref))

    for copy in copies:
        copy.wait()


def pair_map(matrix, source, first_source, first_matrix, *loads):
    shape = matrix.shape
    vmem = pl.BlockSpec(memory_space=pltpu.VMEM)
    hbm = pl.BlockSpec(memory_space=pltpu.HBM)
    return pl.pallas_call(
        pair_body,
        out_shape=[
            jax.ShapeDtypeStruct(shape, BF16),
            jax.ShapeDtypeStruct(shape, F32),
            jax.ShapeDtypeStruct((2, *shape), BF16),
            *(jax.ShapeDtypeStruct(a.shape, BF16) for a in loads),
        ],
        in_specs=[vmem] * 4 + [hbm] * 3,
        out_specs=[vmem] * 6,
        scratch_shapes=[pltpu.SemaphoreType.DMA((3,))],
        compiler_params=pltpu.CompilerParams(vmem_limit_bytes=24 * 2**20),
        cost_estimate=pl.CostEstimate(
            flops=24 * shape[-1] ** 3, bytes_accessed=2**20, transcendentals=0
        ),
    )(
        matrix,
        source,
        first_source,
        first_matrix,
        *(pltpu.with_memory_space_constraint(a, pltpu.HBM) for a in loads),
    )


def hop_body(matrix_ref, source_ref, incoming_ref, green_ref):
    @pl.when(is_at(chip=1, core=1))
    def _():
        put(green_ref, applied(parts(matrix_ref), parts(source_ref), parts(incoming_ref)))


def joined_body(arrived_ref, map_ref, far_ref, out_ref):
    @pl.when(is_at(chip=3, core=1))
    def _():
        put(out_ref, applied(parts(map_ref.at[1]), parts(map_ref.at[0]), parts(far_ref)))

    @pl.when(jnp.logical_not(is_at(chip=3, core=1)))
    def _():
        out_ref[...] = arrived_ref[...]


def lower(shape):
    return lax.broadcasted_iota(jnp.int32, shape, 1) < ROWS // 2


def chunked(part):
    left = part[:, :LANES].reshape(-1, ROWS, LANES)
    right = part[:, LANES:].reshape(-1, ROWS, LANES)
    first = lower(left.shape)
    even = jnp.where(first, left, pltpu.roll(right, ROWS // 2, 1))
    odd = jnp.where(first, pltpu.roll(left, ROWS // 2, 1), right)
    return even, odd


def unchunked(even, odd):
    first = lower(even.shape)
    left = jnp.where(first, even, pltpu.roll(odd, ROWS // 2, 1))
    right = jnp.where(first, pltpu.roll(even, ROWS // 2, 1), odd)
    return left.reshape(-1, LANES), right.reshape(-1, LANES)


def rolled(count, start):
    if start == 0:
        return [(slice(0, count), slice(0, count))]
    return [
        (slice(0, count - start), slice(start, count)),
        (slice(count - start, count), slice(0, start)),
    ]


def last_body(matrix_ref, source_ref, incoming_ref, out_ref):
    green = applied(parts(matrix_ref), parts(source_ref), parts(incoming_ref.at[1]))
    even_real, odd_real = chunked(green[0])
    even_imag, odd_imag = chunked(green[1])
    even = jnp.concatenate([even_real, even_imag], axis=1).astype(BF16)
    odd = jnp.concatenate([odd_real, odd_imag], axis=1).astype(BF16)
    pairs = out_ref.shape[0]
    start = FIRST_OUT // 2
    for target, taken in rolled(pairs, start):
        out_ref[target, 0] = even[taken]
        out_ref[target, 1] = odd[taken]


def spectra_body(chunks_ref, forward_ref, inverse_ref, weights_ref, out_ref, rows_ref):
    count = chunks_ref.shape[0]
    length = weights_ref.shape[0]
    stride = 2 * ROWS
    rows_ref[...] = chunks_ref[...].astype(F32).reshape(rows_ref.shape)
    taken = [rows_ref[pl.ds(i, count, stride=stride), :].astype(BF16) for i in range(stride)]
    values = jnp.concatenate(
        [jnp.concatenate(taken[:ROWS], axis=1), jnp.concatenate(taken[ROWS:], axis=1)], axis=0
    )
    spectrum = dot(forward_ref[...], values) * (count**-0.5)
    order = [2 * (i % 4) + i // 4 for i in range(ROWS)]
    weights = jnp.concatenate(
        [weights_ref[:, LANES * i : LANES * (i + 1)] for i in order], axis=1
    ).astype(F32)
    real, imag = spectrum[:length], spectrum[length:]
    squared_real = ((real * real - imag * imag) * weights).astype(BF16)
    squared_imag = (2.0 * real * imag * weights).astype(BF16)
    result = dot(inverse_ref[...], jnp.concatenate([squared_real, squared_imag], axis=0))
    result = result * (length**-0.5)
    for i in range(ROWS):
        columns = slice(LANES * i, LANES * (i + 1))
        rows_ref[pl.ds(i, count, stride=stride), :] = result[:count, columns]
        rows_ref[pl.ds(i + ROWS, count, stride=stride), :] = result[count:, columns]
    out_ref[...] = rows_ref[...].reshape(out_ref.shape).astype(BF16)


def output_body(chunks_ref, out_ref):
    even = chunks_ref[:, 0].astype(F32)
    odd = chunks_ref[:, 1].astype(F32)
    for part in range(2):
        rows = slice(ROWS * part, ROWS * (part + 1))
        left, right = unchunked(even[:, rows], odd[:, rows])
        value = jnp.concatenate([left, right], axis=1).astype(BF16)
        for taken, target in rolled(value.shape[0], 2 * ROWS // 4 * FIRST_BACK):
            out_ref[part, target] = value[taken]


def phase_table(row_count, column_count, length):
    residue = np.arange(row_count)[:, None] * np.arange(column_count)[None, :] % length
    return residue.astype(np.float32) * np.float32(2.0 * math.pi / length)


def complex_table(real, imag):
    return jnp.asarray(np.block([[real, -imag], [imag, real]]).astype(ml_dtypes.bfloat16))


def tables(count, length):
    phase = np.roll(phase_table(length, count, length), -FIRST_OUT, axis=1)
    forward = complex_table(np.cos(phase), -np.sin(phase))
    phase = np.roll(phase_table(count, length, length), -FIRST_BACK, axis=0)
    inverse = complex_table(np.cos(phase), np.sin(phase))
    return forward, inverse


def spectra(chunks, forward, inverse, weights):
    count = chunks.shape[0]
    length = weights.shape[0]
    return pl.pallas_call(
        spectra_body,
        out_shape=jax.ShapeDtypeStruct(chunks.shape, BF16),
        scratch_shapes=[pltpu.VMEM((count * 2 * ROWS, LANES), F32)],
        compiler_params=pltpu.CompilerParams(vmem_limit_bytes=24 * 2**20),
        cost_estimate=pl.CostEstimate(
            flops=16 * length * count * LANES * ROWS, bytes_accessed=3 * 2**18, transcendentals=0
        ),
    )(chunks, forward, inverse, weights)


def exchanged(chunks, first):
    count = chunks.shape[0]
    group = [(first + i) % count for i in range(count)]
    return lax.all_to_all(
        chunks, "energy", split_axis=0, concat_axis=0, axis_index_groups=[group], tiled=True
    )


def local(lesser_in, retarded, coupling, interaction):
    order = coupling.shape[-1]
    energies = lax.axis_size("energy")
    shape = (2, order, order)
    chunk = (energies, 2 * ROWS, LANES)
    one = 8 * order**3

    matrix, source, sent = prelude(lesser_in[0, 0], retarded[0, 0], coupling[0])
    first_source = lax.all_gather(sent, "core")
    green = call(leading_body, [(shape, BF16)], matrix, source, first_source, flops=2 * one)
    arrived = lax.ppermute(green, SPACE, [(1, 3)])
    first_matrix = lax.all_gather(matrix, "core")
    matrix, source, sent, weights, forward, inverse = pair_map(
        matrix,
        source,
        first_source,
        first_matrix,
        interaction[0],
        *tables(energies, interaction.shape[1]),
    )
    chip_map = lax.ppermute(sent, SPACE, [(5, 7)])
    green = call(hop_body, [(shape, BF16)], matrix, source, arrived, flops=2 * one)
    near = lax.ppermute(green, SPACE, [(3, 5)])
    far = lax.ppermute(green, SPACE, [(3, 7)])
    incoming = call(joined_body, [(shape, BF16)], arrived, chip_map, far, flops=2 * one) + near
    incoming = lax.all_gather(incoming, "core")
    chunks = call(
        last_body,
        [((energies // 2, 2, 2 * ROWS, LANES), BF16)],
        matrix,
        source,
        incoming,
        flops=2 * one,
    )
    chunks = exchanged(chunks.reshape(chunk), FIRST_OUT)
    result = spectra(chunks, forward, inverse, weights)
    returned = exchanged(result, FIRST_BACK)
    out = call(
        output_body,
        [(shape, BF16)],
        returned.reshape(energies // 2, 2, 2 * ROWS, LANES),
    )
    return out.reshape(1, 1, *shape)


def solution(mesh):
    split = Mesh(
        mesh.devices.reshape(mesh.shape["space"] // 2, 2, mesh.shape["energy"]),
        ("chip", "core", "energy"),
    )
    in_specs = (
        P("energy", SPACE, None, None, None),
        P("energy", SPACE, None, None, None),
        P(SPACE, None, None, None),
        P(SPACE, None, "energy"),
    )
    out_specs = P("energy", SPACE, None, None, None)
    return jax.shard_map(local, mesh=split, in_specs=in_specs, out_specs=out_specs, check_vma=False)
```

```python
import functools
import math

import jax
import jax.numpy as jnp
import ml_dtypes
import numpy as np
from jax import lax
from jax.experimental import pallas as pl
from jax.experimental.pallas import tpu as pltpu
from jax.sharding import Mesh
from jax.sharding import PartitionSpec as P

SPACE = ("chip", "core")
BF16 = jnp.bfloat16
F32 = jnp.float32
LANES = 128
ROWS = 8
FIRST_OUT = 42
FIRST_BACK = 42


def dot(left, right):
    return jnp.dot(left, right, preferred_element_type=F32)


def dot_adjoint(left, right):
    return lax.dot_general(left, right, (((1,), (1,)), ((), ())), preferred_element_type=F32)


def product(left, right):
    real_part = dot(
        jnp.concatenate([left[0], -left[1]], axis=1), jnp.concatenate([right[0], right[1]], axis=0)
    )
    imag_part = dot(
        jnp.concatenate([left[0], left[1]], axis=1), jnp.concatenate([right[1], right[0]], axis=0)
    )
    return (real_part, imag_part)


def product_adjoint(left, right):
    right = jnp.concatenate(right, axis=1)
    real_part = dot_adjoint(jnp.concatenate([left[0], left[1]], axis=1), right)
    imag_part = dot_adjoint(jnp.concatenate([left[1], -left[0]], axis=1), right)
    return (real_part, imag_part)


def rounded(pair):
    return (pair[0].astype(BF16), pair[1].astype(BF16))


def parts(ref):
    return (ref[0], ref[1])


def put(ref, pair):
    ref[0] = pair[0].astype(ref.dtype)
    ref[1] = pair[1].astype(ref.dtype)


def applied(matrix, source, green):
    carried = rounded(product(matrix, green))
    grown = product_adjoint(carried, matrix)
    return (source[0] + grown[0], source[1] + grown[1])


def call(body, outs, *operands, flops=0, in_place=False):
    outs = [jax.ShapeDtypeStruct(shape, dtype) for shape, dtype in outs]
    size = sum(math.prod(a.shape) * a.dtype.itemsize for a in [*operands, *outs])
    return pl.pallas_call(
        body,
        out_shape=outs if len(outs) > 1 else outs[0],
        input_output_aliases={len(operands) - 1: 0} if in_place else {},
        compiler_params=pltpu.CompilerParams(vmem_limit_bytes=24 * 2**20),
        cost_estimate=pl.CostEstimate(flops=flops, bytes_accessed=size, transcendentals=0),
    )(*operands)


def prelude_body(
    lesser_hbm, retarded_hbm, coupling_hbm, matrix_ref, source_ref, sent_ref, loaded, semaphores
):
    copies = [
        pltpu.make_async_copy(ref, loaded.at[i], semaphores.at[i])
        for i, ref in enumerate((retarded_hbm, lesser_hbm, coupling_hbm))
    ]
    for copy in copies:
        copy.start()
    copies[0].wait()
    copies[1].wait()
    resolvent = parts(loaded.at[0])
    half = rounded(product(resolvent, parts(loaded.at[1])))
    source = product_adjoint(half, resolvent)
    put(source_ref, source)
    put(sent_ref, source)
    copies[2].wait()
    put(matrix_ref, product(resolvent, parts(loaded.at[2])))


def prelude(lesser_in, retarded, coupling):
    shape = coupling.shape
    return pl.pallas_call(
        prelude_body,
        out_shape=[jax.ShapeDtypeStruct(shape, dtype) for dtype in (BF16, F32, BF16)],
        in_specs=[pl.BlockSpec(memory_space=pltpu.HBM)] * 3,
        out_specs=[pl.BlockSpec(memory_space=pltpu.VMEM)] * 3,
        scratch_shapes=[pltpu.VMEM((3, *shape), BF16), pltpu.SemaphoreType.DMA((3,))],
        compiler_params=pltpu.CompilerParams(vmem_limit_bytes=24 * 2**20),
        cost_estimate=pl.CostEstimate(
            flops=24 * shape[-1] ** 3, bytes_accessed=2**20, transcendentals=0
        ),
    )(*(pltpu.with_memory_space_constraint(a, pltpu.HBM) for a in (lesser_in, retarded, coupling)))


def is_at(**place):
    tests = [lax.axis_index(axis) == index for axis, index in place.items()]
    return functools.reduce(jnp.logical_and, tests)


def leading_body(matrix_ref, source_ref, first_ref, green_ref):
    @pl.when(is_at(chip=0, core=1))
    def _():
        put(green_ref, applied(parts(matrix_ref), parts(source_ref), parts(first_ref.at[0])))


def pair_body(
    source_ref,
    sources_ref,
    matrices_ref,
    weights_hbm,
    forward_hbm,
    inverse_hbm,
    total_ref,
    green_ref,
    map_ref,
    weights_ref,
    forward_ref,
    inverse_ref,
    semaphores,
):
    pairs = ((weights_hbm, weights_ref), (forward_hbm, forward_ref), (inverse_hbm, inverse_ref))
    copies = [pltpu.make_async_copy(*pair, semaphores.at[i]) for i, pair in enumerate(pairs)]
    for copy in copies:
        copy.start()

    def composed(second_source):
        second_matrix = parts(matrices_ref.at[1])
        total = applied(second_matrix, second_source, parts(sources_ref.at[0]))
        put(total_ref, total)
        put(green_ref, total)
        put(map_ref.at[0], total)
        put(map_ref.at[1], product(second_matrix, parts(matrices_ref.at[0])))

    @pl.when(is_at(core=1))
    def _():
        composed(parts(source_ref))

    @pl.when(is_at(core=0))
    def _():
        composed(parts(sources_ref.at[1]))

    for copy in copies:
        copy.wait()


def pair_map(source, sources, matrices, *loads):
    shape = source.shape
    vmem = pl.BlockSpec(memory_space=pltpu.VMEM)
    hbm = pl.BlockSpec(memory_space=pltpu.HBM)
    return pl.pallas_call(
        pair_body,
        out_shape=[
            jax.ShapeDtypeStruct(shape, F32),
            jax.ShapeDtypeStruct(shape, BF16),
            jax.ShapeDtypeStruct((2, *shape), BF16),
            *(jax.ShapeDtypeStruct(a.shape, BF16) for a in loads),
        ],
        in_specs=[vmem] * 3 + [hbm] * 3,
        out_specs=[vmem] * 6,
        scratch_shapes=[pltpu.SemaphoreType.DMA((3,))],
        compiler_params=pltpu.CompilerParams(vmem_limit_bytes=24 * 2**20),
        cost_estimate=pl.CostEstimate(
            flops=24 * shape[-1] ** 3, bytes_accessed=2**20, transcendentals=0
        ),
    )(source, sources, matrices, *(pltpu.with_memory_space_constraint(a, pltpu.HBM) for a in loads))


def hop_body(map_ref, total_ref, arrived_later_ref, arrived_ref, green_ref):
    for core, ref in ((1, arrived_ref), (0, arrived_later_ref)):

        @pl.when(is_at(chip=1, core=core))
        def _():
            put(green_ref, applied(parts(map_ref.at[1]), parts(total_ref), parts(ref)))


def joined_body(arrived_later_ref, arrived_ref, map_ref, far_ref, out_ref):
    @pl.when(is_at(chip=3, core=1))
    def _():
        put(out_ref, applied(parts(map_ref.at[1]), parts(map_ref.at[0]), parts(far_ref)))

    @pl.when(lax.axis_index("chip") != 3)
    def _():
        out_ref[...] = arrived_ref[...] + arrived_later_ref[...]


def lower(shape):
    return lax.broadcasted_iota(jnp.int32, shape, 1) < ROWS // 2


def chunked(part):
    left = part[:, :LANES].reshape(-1, ROWS, LANES)
    right = part[:, LANES:].reshape(-1, ROWS, LANES)
    first = lower(left.shape)
    even = jnp.where(first, left, pltpu.roll(right, ROWS // 2, 1))
    odd = jnp.where(first, pltpu.roll(left, ROWS // 2, 1), right)
    return even, odd


def unchunked(even, odd):
    first = lower(even.shape)
    left = jnp.where(first, even, pltpu.roll(odd, ROWS // 2, 1))
    right = jnp.where(first, pltpu.roll(even, ROWS // 2, 1), odd)
    return left.reshape(-1, LANES), right.reshape(-1, LANES)


def rolled(count, start):
    if start == 0:
        return [(slice(0, count), slice(0, count))]
    return [
        (slice(0, count - start), slice(start, count)),
        (slice(count - start, count), slice(0, start)),
    ]


def cut(matrix, source, incoming, out_ref):
    green = applied(matrix, source, incoming)
    even_real, odd_real = chunked(green[0])
    even_imag, odd_imag = chunked(green[1])
    even = jnp.concatenate([even_real, even_imag], axis=1).astype(BF16)
    odd = jnp.concatenate([odd_real, odd_imag], axis=1).astype(BF16)
    for target, taken in rolled(out_ref.shape[0], FIRST_OUT // 2):
        out_ref[target, 0] = even[taken]
        out_ref[target, 1] = odd[taken]


def entered(incoming_ref, near_ref):
    total = incoming_ref[...] + near_ref[...]
    return (total[0], total[1])


def last_body(map_ref, total_ref, incoming_ref, near_ref, out_ref):
    @pl.when(is_at(core=1))
    def _():
        incoming = entered(incoming_ref, near_ref)
        cut(parts(map_ref.at[1]), parts(total_ref), incoming, out_ref)


def last_later_body(
    matrix_ref, source_ref, map_ref, far_ref, incoming_ref, near_ref, before_ref, out_ref
):
    in_last_chip = lax.axis_index("chip") == 3
    on_first_core = lax.axis_index("core") == 0

    @pl.when(on_first_core & jnp.logical_not(in_last_chip))
    def _():
        incoming = entered(incoming_ref, near_ref)
        cut(parts(matrix_ref), parts(source_ref), incoming, out_ref)

    @pl.when(on_first_core & in_last_chip)
    def _():
        map_source, map_matrix = parts(map_ref.at[0]), parts(map_ref.at[1])
        incoming = rounded(applied(map_matrix, map_source, parts(far_ref)))
        cut(parts(matrix_ref), parts(source_ref), incoming, out_ref)


def spectra_body(chunks_ref, forward_ref, inverse_ref, weights_ref, out_ref, rows_ref):
    count = chunks_ref.shape[0]
    length = weights_ref.shape[0]
    stride = 2 * ROWS
    rows_ref[...] = chunks_ref[...].astype(F32).reshape(rows_ref.shape)
    taken = [rows_ref[pl.ds(i, count, stride=stride), :].astype(BF16) for i in range(stride)]
    values = jnp.concatenate(
        [jnp.concatenate(taken[:ROWS], axis=1), jnp.concatenate(taken[ROWS:], axis=1)], axis=0
    )
    spectrum = dot(forward_ref[...], values) * (count**-0.5)
    order = [2 * (i % 4) + i // 4 for i in range(ROWS)]
    weights = jnp.concatenate(
        [weights_ref[:, LANES * i : LANES * (i + 1)] for i in order], axis=1
    ).astype(F32)
    real, imag = spectrum[:length], spectrum[length:]
    squared_real = ((real * real - imag * imag) * weights).astype(BF16)
    squared_imag = (2.0 * real * imag * weights).astype(BF16)
    result = dot(inverse_ref[...], jnp.concatenate([squared_real, squared_imag], axis=0))
    result = result * (length**-0.5)
    for i in range(ROWS):
        columns = slice(LANES * i, LANES * (i + 1))
        rows_ref[pl.ds(i, count, stride=stride), :] = result[:count, columns]
        rows_ref[pl.ds(i + ROWS, count, stride=stride), :] = result[count:, columns]
    out_ref[...] = rows_ref[...].reshape(out_ref.shape).astype(BF16)


def output_body(chunks_ref, out_hbm, out_ref, semaphores):
    even = chunks_ref[:, 0].astype(F32)
    odd = chunks_ref[:, 1].astype(F32)
    copies = []
    for part in range(2):
        rows = slice(ROWS * part, ROWS * (part + 1))
        left, right = unchunked(even[:, rows], odd[:, rows])
        value = jnp.concatenate([left, right], axis=1).astype(BF16)
        for taken, target in rolled(value.shape[0], 2 * ROWS // 4 * FIRST_BACK):
            out_ref[part, target] = value[taken]
        copy = pltpu.make_async_copy(out_ref.at[part], out_hbm.at[part], semaphores.at[part])
        copy.start()
        copies.append(copy)
    for copy in copies:
        copy.wait()


def output(chunks, shape):
    return pl.pallas_call(
        output_body,
        out_shape=jax.ShapeDtypeStruct(shape, BF16),
        out_specs=pl.BlockSpec(memory_space=pltpu.HBM),
        scratch_shapes=[pltpu.VMEM(shape, BF16), pltpu.SemaphoreType.DMA((2,))],
        compiler_params=pltpu.CompilerParams(vmem_limit_bytes=24 * 2**20),
        cost_estimate=pl.CostEstimate(flops=0, bytes_accessed=2**19, transcendentals=0),
    )(chunks)


def phase_table(row_count, column_count, length):
    residue = np.arange(row_count)[:, None] * np.arange(column_count)[None, :] % length
    return residue.astype(np.float32) * np.float32(2.0 * math.pi / length)


def complex_table(real, imag):
    return jnp.asarray(np.block([[real, -imag], [imag, real]]).astype(ml_dtypes.bfloat16))


def tables(count, length):
    phase = np.roll(phase_table(length, count, length), -FIRST_OUT, axis=1)
    forward = complex_table(np.cos(phase), -np.sin(phase))
    phase = np.roll(phase_table(count, length, length), -FIRST_BACK, axis=0)
    inverse = complex_table(np.cos(phase), np.sin(phase))
    return forward, inverse


def spectra(chunks, forward, inverse, weights):
    count = chunks.shape[0]
    length = weights.shape[0]
    return pl.pallas_call(
        spectra_body,
        out_shape=jax.ShapeDtypeStruct(chunks.shape, BF16),
        scratch_shapes=[pltpu.VMEM((count * 2 * ROWS, LANES), F32)],
        compiler_params=pltpu.CompilerParams(vmem_limit_bytes=24 * 2**20),
        cost_estimate=pl.CostEstimate(
            flops=16 * length * count * LANES * ROWS, bytes_accessed=3 * 2**18, transcendentals=0
        ),
    )(chunks, forward, inverse, weights)


def after(array, other):
    return lax.optimization_barrier((array, other))[0]


def exchanged(chunks, first):
    count = chunks.shape[0]
    group = [(first + i) % count for i in range(count)]
    return lax.all_to_all(
        chunks, "energy", split_axis=0, concat_axis=0, axis_index_groups=[group], tiled=True
    )


def local(lesser_in, retarded, coupling, interaction):
    order = coupling.shape[-1]
    energies = lax.axis_size("energy")
    shape = (2, order, order)
    chunk = (energies, 2 * ROWS, LANES)
    one = 8 * order**3

    matrix, source, sent = prelude(lesser_in[0, 0], retarded[0, 0], coupling[0])
    sources = lax.all_gather(sent, "core")
    green = call(leading_body, [(shape, BF16)], matrix, source, sources, flops=60 * one)
    arrived = lax.ppermute(green, SPACE, [(1, 3)])
    matrices = lax.all_gather(matrix, "core")
    total, green, chip_map, weights, forward, inverse = pair_map(
        source,
        sources,
        matrices,
        interaction[0],
        *tables(energies, interaction.shape[1]),
    )
    map_arrived = lax.ppermute(chip_map, SPACE, [(5, 7)])
    arrived_later = lax.ppermute(after(green, arrived), SPACE, [(0, 2)])
    green = call(
        hop_body, [(shape, BF16)], chip_map, total, arrived_later, arrived, flops=60 * one
    )
    near = lax.ppermute(green, SPACE, [(3, 5), (2, 4)])
    far = lax.ppermute(green, SPACE, [(3, 7), (2, 6)])
    map_later = lax.ppermute(after(map_arrived, green), SPACE, [(7, 6)])
    incoming = call(
        joined_body,
        [(shape, BF16)],
        arrived_later,
        arrived,
        map_arrived,
        far,
        flops=60 * one,
    )
    cut_shape = (energies // 2, 2, 2 * ROWS, LANES)
    chunks = call(
        last_body, [(cut_shape, BF16)], chip_map, total, incoming, near, flops=2 * one
    )
    chunks = call(
        last_later_body,
        [(cut_shape, BF16)],
        matrix,
        source,
        map_later,
        far,
        incoming,
        near,
        chunks,
        flops=2 * one,
        in_place=True,
    )
    chunks = exchanged(chunks.reshape(chunk), FIRST_OUT)
    result = spectra(chunks, forward, inverse, weights)
    returned = exchanged(result, FIRST_BACK)
    out = output(returned.reshape(energies // 2, 2, 2 * ROWS, LANES), shape)
    return out.reshape(1, 1, *shape)


def solution(mesh):
    split = Mesh(
        mesh.devices.reshape(mesh.shape["space"] // 2, 2, mesh.shape["energy"]),
        ("chip", "core", "energy"),
    )
    in_specs = (
        P("energy", SPACE, None, None, None),
        P("energy", SPACE, None, None, None),
        P(SPACE, None, None, None),
        P(SPACE, None, "energy"),
    )
    out_specs = P("energy", SPACE, None, None, None)
    return jax.shard_map(local, mesh=split, in_specs=in_specs, out_specs=out_specs, check_vma=False)
```

```python
import functools
import math

import jax
import jax.numpy as jnp
import ml_dtypes
import numpy as np
from jax import lax
from jax.experimental import pallas as pl
from jax.experimental.pallas import tpu as pltpu
from jax.sharding import Mesh
from jax.sharding import PartitionSpec as P

SPACE = ("chip", "core")
BF16 = jnp.bfloat16
F32 = jnp.float32
LANES = 128
ROWS = 8
FIRST_OUT = 42
FIRST_BACK = 42


def dot(left, right):
    return jnp.dot(left, right, preferred_element_type=F32)


def dot_adjoint(left, right):
    return lax.dot_general(left, right, (((1,), (1,)), ((), ())), preferred_element_type=F32)


def product(left, right):
    real_part = dot(
        jnp.concatenate([left[0], -left[1]], axis=1), jnp.concatenate([right[0], right[1]], axis=0)
    )
    imag_part = dot(
        jnp.concatenate([left[0], left[1]], axis=1), jnp.concatenate([right[1], right[0]], axis=0)
    )
    return (real_part, imag_part)


def product_adjoint(left, right):
    right = jnp.concatenate(right, axis=1)
    real_part = dot_adjoint(jnp.concatenate([left[0], left[1]], axis=1), right)
    imag_part = dot_adjoint(jnp.concatenate([left[1], -left[0]], axis=1), right)
    return (real_part, imag_part)


def rounded(pair):
    return (pair[0].astype(BF16), pair[1].astype(BF16))


def parts(ref):
    return (ref[0], ref[1])


def put(ref, pair):
    ref[0] = pair[0].astype(ref.dtype)
    ref[1] = pair[1].astype(ref.dtype)


def applied(matrix, source, green):
    carried = rounded(product(matrix, green))
    grown = product_adjoint(carried, matrix)
    return (source[0] + grown[0], source[1] + grown[1])


def call(body, outs, *operands, flops=0, in_place=False):
    outs = [jax.ShapeDtypeStruct(shape, dtype) for shape, dtype in outs]
    size = sum(math.prod(a.shape) * a.dtype.itemsize for a in [*operands, *outs])
    return pl.pallas_call(
        body,
        out_shape=outs if len(outs) > 1 else outs[0],
        input_output_aliases={len(operands) - 1: 0} if in_place else {},
        compiler_params=pltpu.CompilerParams(vmem_limit_bytes=24 * 2**20),
        cost_estimate=pl.CostEstimate(flops=flops, bytes_accessed=size, transcendentals=0),
    )(*operands)


def prelude_body(
    lesser_hbm, retarded_hbm, coupling_hbm, matrix_ref, source_ref, sent_ref, loaded, semaphores
):
    copies = [
        pltpu.make_async_copy(ref, loaded.at[i], semaphores.at[i])
        for i, ref in enumerate((retarded_hbm, lesser_hbm, coupling_hbm))
    ]
    for copy in copies:
        copy.start()
    copies[0].wait()
    copies[1].wait()
    resolvent = parts(loaded.at[0])
    half = rounded(product(resolvent, parts(loaded.at[1])))
    source = product_adjoint(half, resolvent)
    put(source_ref, source)
    put(sent_ref, source)
    copies[2].wait()
    put(matrix_ref, product(resolvent, parts(loaded.at[2])))


def prelude(lesser_in, retarded, coupling):
    shape = coupling.shape
    return pl.pallas_call(
        prelude_body,
        out_shape=[jax.ShapeDtypeStruct(shape, dtype) for dtype in (BF16, F32, BF16)],
        in_specs=[pl.BlockSpec(memory_space=pltpu.HBM)] * 3,
        out_specs=[pl.BlockSpec(memory_space=pltpu.VMEM)] * 3,
        scratch_shapes=[pltpu.VMEM((3, *shape), BF16), pltpu.SemaphoreType.DMA((3,))],
        compiler_params=pltpu.CompilerParams(vmem_limit_bytes=24 * 2**20),
        cost_estimate=pl.CostEstimate(
            flops=24 * shape[-1] ** 3, bytes_accessed=2**20, transcendentals=0
        ),
    )(*(pltpu.with_memory_space_constraint(a, pltpu.HBM) for a in (lesser_in, retarded, coupling)))


def is_at(**place):
    tests = [lax.axis_index(axis) == index for axis, index in place.items()]
    return functools.reduce(jnp.logical_and, tests)


def leading_body(matrix_ref, source_ref, first_ref, green_ref):
    @pl.when(is_at(chip=0, core=1))
    def _():
        put(green_ref, applied(parts(matrix_ref), parts(source_ref), parts(first_ref.at[0])))


def pair_body(
    source_ref,
    sources_ref,
    matrices_ref,
    weights_hbm,
    forward_hbm,
    inverse_hbm,
    total_ref,
    map_ref,
    weights_ref,
    forward_ref,
    inverse_ref,
    semaphores,
):
    pairs = ((weights_hbm, weights_ref), (forward_hbm, forward_ref), (inverse_hbm, inverse_ref))
    copies = [pltpu.make_async_copy(*pair, semaphores.at[i]) for i, pair in enumerate(pairs)]
    for copy in copies:
        copy.start()

    def composed(second_source):
        second_matrix = parts(matrices_ref.at[1])
        total = applied(second_matrix, second_source, parts(sources_ref.at[0]))
        put(total_ref, total)
        put(map_ref.at[0], total)
        put(map_ref.at[1], product(second_matrix, parts(matrices_ref.at[0])))

    @pl.when(is_at(core=1))
    def _():
        composed(parts(source_ref))

    @pl.when(is_at(core=0))
    def _():
        composed(parts(sources_ref.at[1]))

    for copy in copies:
        copy.wait()


def pair_map(source, sources, matrices, *loads):
    shape = source.shape
    vmem = pl.BlockSpec(memory_space=pltpu.VMEM)
    hbm = pl.BlockSpec(memory_space=pltpu.HBM)
    return pl.pallas_call(
        pair_body,
        out_shape=[
            jax.ShapeDtypeStruct(shape, F32),
            jax.ShapeDtypeStruct((2, *shape), BF16),
            *(jax.ShapeDtypeStruct(a.shape, BF16) for a in loads),
        ],
        in_specs=[vmem] * 3 + [hbm] * 3,
        out_specs=[vmem] * 5,
        scratch_shapes=[pltpu.SemaphoreType.DMA((3,))],
        compiler_params=pltpu.CompilerParams(vmem_limit_bytes=24 * 2**20),
        cost_estimate=pl.CostEstimate(
            flops=24 * shape[-1] ** 3, bytes_accessed=2**20, transcendentals=0
        ),
    )(source, sources, matrices, *(pltpu.with_memory_space_constraint(a, pltpu.HBM) for a in loads))


def hop_body(map_ref, total_ref, arrived_ref, green_ref):
    @pl.when(is_at(chip=1, core=1))
    def _():
        put(green_ref, applied(parts(map_ref.at[1]), parts(total_ref), parts(arrived_ref)))


def hop_later_body(map_ref, total_ref, arrived_ref, green_ref):
    @pl.when(is_at(chip=1, core=0))
    def _():
        put(green_ref, applied(parts(map_ref.at[1]), parts(total_ref), parts(arrived_ref.at[1])))


def joined_body(arrived_ref, map_ref, far_ref, out_ref):
    @pl.when(is_at(chip=3, core=1))
    def _():
        put(out_ref, applied(parts(map_ref.at[1]), parts(map_ref.at[0]), parts(far_ref)))

    @pl.when(lax.axis_index("chip") != 3)
    def _():
        out_ref[...] = arrived_ref[...]


def lower(shape):
    return lax.broadcasted_iota(jnp.int32, shape, 1) < ROWS // 2


def chunked(part):
    left = part[:, :LANES].reshape(-1, ROWS, LANES)
    right = part[:, LANES:].reshape(-1, ROWS, LANES)
    first = lower(left.shape)
    even = jnp.where(first, left, pltpu.roll(right, ROWS // 2, 1))
    odd = jnp.where(first, pltpu.roll(left, ROWS // 2, 1), right)
    return even, odd


def unchunked(even, odd):
    first = lower(even.shape)
    left = jnp.where(first, even, pltpu.roll(odd, ROWS // 2, 1))
    right = jnp.where(first, pltpu.roll(even, ROWS // 2, 1), odd)
    return left.reshape(-1, LANES), right.reshape(-1, LANES)


def rolled(count, start):
    if start == 0:
        return [(slice(0, count), slice(0, count))]
    return [
        (slice(0, count - start), slice(start, count)),
        (slice(count - start, count), slice(0, start)),
    ]


def cut(matrix, source, incoming, out_ref):
    green = applied(matrix, source, incoming)
    even_real, odd_real = chunked(green[0])
    even_imag, odd_imag = chunked(green[1])
    even = jnp.concatenate([even_real, even_imag], axis=1).astype(BF16)
    odd = jnp.concatenate([odd_real, odd_imag], axis=1).astype(BF16)
    for target, taken in rolled(out_ref.shape[0], FIRST_OUT // 2):
        out_ref[target, 0] = even[taken]
        out_ref[target, 1] = odd[taken]


def entered(incoming_ref, near_ref):
    return (incoming_ref[0] + near_ref[0], incoming_ref[1] + near_ref[1])


def last_body(map_ref, total_ref, incoming_ref, near_ref, out_ref):
    @pl.when(is_at(core=1))
    def _():
        incoming = entered(incoming_ref, near_ref)
        cut(parts(map_ref.at[1]), parts(total_ref), incoming, out_ref)


def last_later_body(
    matrix_ref, source_ref, map_ref, far_ref, incoming_ref, near_ref, before_ref, out_ref
):
    in_last_chip = lax.axis_index("chip") == 3
    on_first_core = lax.axis_index("core") == 0

    @pl.when(on_first_core & jnp.logical_not(in_last_chip))
    def _():
        incoming = entered(incoming_ref.at[1], near_ref)
        cut(parts(matrix_ref), parts(source_ref), incoming, out_ref)

    @pl.when(on_first_core & in_last_chip)
    def _():
        map_source, map_matrix = parts(map_ref.at[0]), parts(map_ref.at[1])
        incoming = rounded(applied(map_matrix, map_source, parts(far_ref)))
        cut(parts(matrix_ref), parts(source_ref), incoming, out_ref)


def spectra_body(chunks_ref, forward_ref, inverse_ref, weights_ref, out_ref, rows_ref):
    count = chunks_ref.shape[0]
    length = weights_ref.shape[0]
    stride = 2 * ROWS
    rows_ref[...] = chunks_ref[...].astype(F32).reshape(rows_ref.shape)
    taken = [rows_ref[pl.ds(i, count, stride=stride), :].astype(BF16) for i in range(stride)]
    values = jnp.concatenate(
        [jnp.concatenate(taken[:ROWS], axis=1), jnp.concatenate(taken[ROWS:], axis=1)], axis=0
    )
    spectrum = dot(forward_ref[...], values) * (count**-0.5)
    order = [2 * (i % 4) + i // 4 for i in range(ROWS)]
    weights = jnp.concatenate(
        [weights_ref[:, LANES * i : LANES * (i + 1)] for i in order], axis=1
    ).astype(F32)
    real, imag = spectrum[:length], spectrum[length:]
    squared_real = ((real * real - imag * imag) * weights).astype(BF16)
    squared_imag = (2.0 * real * imag * weights).astype(BF16)
    result = dot(inverse_ref[...], jnp.concatenate([squared_real, squared_imag], axis=0))
    result = result * (length**-0.5)
    for i in range(ROWS):
        columns = slice(LANES * i, LANES * (i + 1))
        rows_ref[pl.ds(i, count, stride=stride), :] = result[:count, columns]
        rows_ref[pl.ds(i + ROWS, count, stride=stride), :] = result[count:, columns]
    out_ref[...] = rows_ref[...].reshape(out_ref.shape).astype(BF16)


def output_body(chunks_ref, out_hbm, out_ref, semaphores):
    even = chunks_ref[:, 0].astype(F32)
    odd = chunks_ref[:, 1].astype(F32)
    copies = []
    for part in range(2):
        rows = slice(ROWS * part, ROWS * (part + 1))
        left, right = unchunked(even[:, rows], odd[:, rows])
        value = jnp.concatenate([left, right], axis=1)
        rest = value.shape[0] - ROWS // 2 * FIRST_BACK
        out_ref[part] = jnp.concatenate([value[rest:], value[:rest]], axis=0).astype(BF16)
        copy = pltpu.make_async_copy(out_ref.at[part], out_hbm.at[part], semaphores.at[part])
        copy.start()
        copies.append(copy)
    for copy in copies:
        copy.wait()


def output(chunks, shape):
    return pl.pallas_call(
        output_body,
        out_shape=jax.ShapeDtypeStruct(shape, BF16),
        out_specs=pl.BlockSpec(memory_space=pltpu.HBM),
        scratch_shapes=[pltpu.VMEM(shape, BF16), pltpu.SemaphoreType.DMA((2,))],
        compiler_params=pltpu.CompilerParams(vmem_limit_bytes=24 * 2**20),
        cost_estimate=pl.CostEstimate(flops=0, bytes_accessed=2**19, transcendentals=0),
    )(chunks)


def phase_table(row_count, column_count, length):
    residue = np.arange(row_count)[:, None] * np.arange(column_count)[None, :] % length
    return residue.astype(np.float32) * np.float32(2.0 * math.pi / length)


def complex_table(real, imag):
    return jnp.asarray(np.block([[real, -imag], [imag, real]]).astype(ml_dtypes.bfloat16))


def tables(count, length):
    phase = np.roll(phase_table(length, count, length), -FIRST_OUT, axis=1)
    forward = complex_table(np.cos(phase), -np.sin(phase))
    phase = np.roll(phase_table(count, length, length), -FIRST_BACK, axis=0)
    inverse = complex_table(np.cos(phase), np.sin(phase))
    return forward, inverse


def spectra(chunks, forward, inverse, weights):
    count = chunks.shape[0]
    length = weights.shape[0]
    return pl.pallas_call(
        spectra_body,
        out_shape=jax.ShapeDtypeStruct(chunks.shape, BF16),
        scratch_shapes=[pltpu.VMEM((count * 2 * ROWS, LANES), F32)],
        compiler_params=pltpu.CompilerParams(vmem_limit_bytes=24 * 2**20),
        cost_estimate=pl.CostEstimate(
            flops=16 * length * count * LANES * ROWS, bytes_accessed=3 * 2**18, transcendentals=0
        ),
    )(chunks, forward, inverse, weights)


def after(array, other):
    return lax.optimization_barrier((array, other))[0]


def exchanged(chunks, first):
    count = chunks.shape[0]
    group = [(first + i) % count for i in range(count)]
    return lax.all_to_all(
        chunks, "energy", split_axis=0, concat_axis=0, axis_index_groups=[group], tiled=True
    )


def local(lesser_in, retarded, coupling, interaction):
    order = coupling.shape[-1]
    energies = lax.axis_size("energy")
    shape = (2, order, order)
    chunk = (energies, 2 * ROWS, LANES)
    one = 8 * order**3

    matrix, source, sent = prelude(lesser_in[0, 0], retarded[0, 0], coupling[0])
    sources = lax.all_gather(sent, "core")
    green = call(leading_body, [(shape, BF16)], matrix, source, sources, flops=2 * one)
    arrived = lax.ppermute(green, SPACE, [(1, 3)])
    matrices = lax.all_gather(matrix, "core")
    total, chip_map, weights, forward, inverse = pair_map(
        source,
        sources,
        matrices,
        interaction[0],
        *tables(energies, interaction.shape[1]),
    )
    map_arrived = lax.ppermute(chip_map, SPACE, [(5, 7)])
    green = call(
        hop_body, [(shape, BF16)], chip_map, total, arrived, flops=2 * one
    )
    near = lax.ppermute(green, SPACE, [(3, 5)])
    far = lax.ppermute(green, SPACE, [(3, 7)])
    arrived_later = lax.all_gather(after(arrived, green), "core")
    green = call(
        hop_later_body,
        [(shape, BF16)],
        chip_map,
        total,
        arrived_later,
        flops=2 * one,
    )
    near_later = lax.ppermute(green, SPACE, [(2, 4)])
    far_later = lax.ppermute(green, SPACE, [(2, 6)])
    map_later = lax.ppermute(map_arrived, SPACE, [(7, 6)])
    incoming = call(
        joined_body, [(shape, BF16)], arrived, map_arrived, far, flops=60 * one
    )
    cut_shape = (energies // 2, 2, 2 * ROWS, LANES)
    chunks = call(
        last_body, [(cut_shape, BF16)], chip_map, total, incoming, near, flops=2 * one
    )
    chunks = call(
        last_later_body,
        [(cut_shape, BF16)],
        matrix,
        source,
        map_later,
        far_later,
        arrived_later,
        near_later,
        chunks,
        flops=2 * one,
        in_place=True,
    )
    chunks = exchanged(chunks.reshape(chunk), FIRST_OUT)
    result = spectra(chunks, forward, inverse, weights)
    returned = exchanged(result, FIRST_BACK)
    out = output(returned.reshape(energies // 2, 2, 2 * ROWS, LANES), shape)
    return out.reshape(1, 1, *shape)


def solution(mesh):
    split = Mesh(
        mesh.devices.reshape(mesh.shape["space"] // 2, 2, mesh.shape["energy"]),
        ("chip", "core", "energy"),
    )
    in_specs = (
        P("energy", SPACE, None, None, None),
        P("energy", SPACE, None, None, None),
        P(SPACE, None, None, None),
        P(SPACE, None, "energy"),
    )
    out_specs = P("energy", SPACE, None, None, None)
    return jax.shard_map(local, mesh=split, in_specs=in_specs, out_specs=out_specs, check_vma=False)
```

```python
import functools
import math

import jax
import jax.numpy as jnp
import ml_dtypes
import numpy as np
from jax import lax
from jax.experimental import pallas as pl
from jax.experimental.pallas import tpu as pltpu
from jax.sharding import Mesh
from jax.sharding import PartitionSpec as P

SPACE = ("chip", "core")
BF16 = jnp.bfloat16
F32 = jnp.float32
LANES = 128
ROWS = 8
FIRST_OUT = 46
FIRST_BACK = 34


def dot(left, right):
    return jnp.dot(left, right, preferred_element_type=F32)


def dot_adjoint(left, right):
    return lax.dot_general(left, right, (((1,), (1,)), ((), ())), preferred_element_type=F32)


def product(left, right):
    real_part = dot(
        jnp.concatenate([left[0], -left[1]], axis=1), jnp.concatenate([right[0], right[1]], axis=0)
    )
    imag_part = dot(
        jnp.concatenate([left[0], left[1]], axis=1), jnp.concatenate([right[1], right[0]], axis=0)
    )
    return (real_part, imag_part)


def product_adjoint(left, right):
    right = jnp.concatenate(right, axis=1)
    real_part = dot_adjoint(jnp.concatenate([left[0], left[1]], axis=1), right)
    imag_part = dot_adjoint(jnp.concatenate([left[1], -left[0]], axis=1), right)
    return (real_part, imag_part)


def rounded(pair):
    return (pair[0].astype(BF16), pair[1].astype(BF16))


def parts(ref):
    return (ref[0], ref[1])


def put(ref, pair):
    ref[0] = pair[0].astype(ref.dtype)
    ref[1] = pair[1].astype(ref.dtype)


def applied(matrix, source, green):
    carried = rounded(product(matrix, green))
    grown = product_adjoint(carried, matrix)
    return (source[0] + grown[0], source[1] + grown[1])


def call(body, outs, *operands, flops=0, in_place=False):
    outs = [jax.ShapeDtypeStruct(shape, dtype) for shape, dtype in outs]
    size = sum(math.prod(a.shape) * a.dtype.itemsize for a in [*operands, *outs])
    return pl.pallas_call(
        body,
        out_shape=outs if len(outs) > 1 else outs[0],
        input_output_aliases={len(operands) - 1: 0} if in_place else {},
        compiler_params=pltpu.CompilerParams(vmem_limit_bytes=24 * 2**20),
        cost_estimate=pl.CostEstimate(flops=flops, bytes_accessed=size, transcendentals=0),
    )(*operands)


def prelude_body(
    lesser_hbm, retarded_hbm, coupling_hbm, matrix_ref, source_ref, sent_ref, loaded, semaphores
):
    copies = [
        pltpu.make_async_copy(ref, loaded.at[i], semaphores.at[i])
        for i, ref in enumerate((retarded_hbm, lesser_hbm, coupling_hbm))
    ]
    for copy in copies:
        copy.start()
    copies[0].wait()
    copies[1].wait()
    resolvent = parts(loaded.at[0])
    half = rounded(product(resolvent, parts(loaded.at[1])))
    source = product_adjoint(half, resolvent)
    put(source_ref, source)
    put(sent_ref, source)
    copies[2].wait()
    put(matrix_ref, product(resolvent, parts(loaded.at[2])))


def prelude(lesser_in, retarded, coupling):
    shape = coupling.shape
    return pl.pallas_call(
        prelude_body,
        out_shape=[jax.ShapeDtypeStruct(shape, dtype) for dtype in (BF16, F32, BF16)],
        in_specs=[pl.BlockSpec(memory_space=pltpu.HBM)] * 3,
        out_specs=[pl.BlockSpec(memory_space=pltpu.VMEM)] * 3,
        scratch_shapes=[pltpu.VMEM((3, *shape), BF16), pltpu.SemaphoreType.DMA((3,))],
        compiler_params=pltpu.CompilerParams(vmem_limit_bytes=24 * 2**20),
        cost_estimate=pl.CostEstimate(
            flops=24 * shape[-1] ** 3, bytes_accessed=2**20, transcendentals=0
        ),
    )(*(pltpu.with_memory_space_constraint(a, pltpu.HBM) for a in (lesser_in, retarded, coupling)))


def is_at(**place):
    tests = [lax.axis_index(axis) == index for axis, index in place.items()]
    return functools.reduce(jnp.logical_and, tests)


def leading_body(matrix_ref, source_ref, first_ref, green_ref):
    @pl.when(is_at(chip=0, core=1))
    def _():
        put(green_ref, applied(parts(matrix_ref), parts(source_ref), parts(first_ref.at[0])))


def pair_body(
    source_ref,
    sources_ref,
    matrices_ref,
    weights_hbm,
    forward_hbm,
    inverse_hbm,
    total_ref,
    map_ref,
    weights_ref,
    forward_ref,
    inverse_ref,
    semaphores,
):
    pairs = ((weights_hbm, weights_ref), (forward_hbm, forward_ref), (inverse_hbm, inverse_ref))
    copies = [pltpu.make_async_copy(*pair, semaphores.at[i]) for i, pair in enumerate(pairs)]
    for copy in copies:
        copy.start()

    def composed(second_source):
        second_matrix = parts(matrices_ref.at[1])
        total = applied(second_matrix, second_source, parts(sources_ref.at[0]))
        put(total_ref, total)
        put(map_ref.at[0], total)
        put(map_ref.at[1], product(second_matrix, parts(matrices_ref.at[0])))

    @pl.when(is_at(core=1))
    def _():
        composed(parts(source_ref))

    @pl.when(is_at(core=0))
    def _():
        composed(parts(sources_ref.at[1]))

    for copy in copies:
        copy.wait()


def pair_map(source, sources, matrices, *loads):
    shape = source.shape
    vmem = pl.BlockSpec(memory_space=pltpu.VMEM)
    hbm = pl.BlockSpec(memory_space=pltpu.HBM)
    return pl.pallas_call(
        pair_body,
        out_shape=[
            jax.ShapeDtypeStruct(shape, F32),
            jax.ShapeDtypeStruct((2, *shape), BF16),
            *(jax.ShapeDtypeStruct(a.shape, BF16) for a in loads),
        ],
        in_specs=[vmem] * 3 + [hbm] * 3,
        out_specs=[vmem] * 5,
        scratch_shapes=[pltpu.SemaphoreType.DMA((3,))],
        compiler_params=pltpu.CompilerParams(vmem_limit_bytes=24 * 2**20),
        cost_estimate=pl.CostEstimate(
            flops=24 * shape[-1] ** 3, bytes_accessed=2**20, transcendentals=0
        ),
    )(source, sources, matrices, *(pltpu.with_memory_space_constraint(a, pltpu.HBM) for a in loads))


def hop_body(map_ref, total_ref, arrived_ref, green_ref):
    @pl.when(is_at(chip=1, core=1))
    def _():
        put(green_ref, applied(parts(map_ref.at[1]), parts(total_ref), parts(arrived_ref)))


def hop_later_body(map_ref, total_ref, arrived_ref, green_ref):
    @pl.when(is_at(chip=1, core=0))
    def _():
        put(green_ref, applied(parts(map_ref.at[1]), parts(total_ref), parts(arrived_ref.at[1])))


def joined_body(arrived_ref, map_ref, far_ref, out_ref):
    @pl.when(is_at(chip=3, core=1))
    def _():
        put(out_ref, applied(parts(map_ref.at[1]), parts(map_ref.at[0]), parts(far_ref)))

    @pl.when(lax.axis_index("chip") != 3)
    def _():
        out_ref[...] = arrived_ref[...]


def lower(shape):
    return lax.broadcasted_iota(jnp.int32, shape, 1) < ROWS // 2


def chunked(part):
    left = part[:, :LANES].reshape(-1, ROWS, LANES)
    right = part[:, LANES:].reshape(-1, ROWS, LANES)
    first = lower(left.shape)
    even = jnp.where(first, left, pltpu.roll(right, ROWS // 2, 1))
    odd = jnp.where(first, pltpu.roll(left, ROWS // 2, 1), right)
    return even, odd


def unchunked(even, odd):
    first = lower(even.shape)
    left = jnp.where(first, even, pltpu.roll(odd, ROWS // 2, 1))
    right = jnp.where(first, pltpu.roll(even, ROWS // 2, 1), odd)
    return left.reshape(-1, LANES), right.reshape(-1, LANES)


def rolled(count, start):
    if start == 0:
        return [(slice(0, count), slice(0, count))]
    return [
        (slice(0, count - start), slice(start, count)),
        (slice(count - start, count), slice(0, start)),
    ]


def cut(matrix, source, incoming, out_ref):
    green = applied(matrix, source, incoming)
    even_real, odd_real = chunked(green[0])
    even_imag, odd_imag = chunked(green[1])
    even = jnp.concatenate([even_real, even_imag], axis=1).astype(BF16)
    odd = jnp.concatenate([odd_real, odd_imag], axis=1).astype(BF16)
    for target, taken in rolled(out_ref.shape[0], FIRST_OUT // 2):
        out_ref[target, 0] = even[taken]
        out_ref[target, 1] = odd[taken]


def entered(incoming_ref, near_ref):
    return (incoming_ref[0] + near_ref[0], incoming_ref[1] + near_ref[1])


def last_body(map_ref, total_ref, incoming_ref, near_ref, out_ref):
    @pl.when(is_at(core=1))
    def _():
        incoming = entered(incoming_ref, near_ref)
        cut(parts(map_ref.at[1]), parts(total_ref), incoming, out_ref)


def last_later_body(
    matrix_ref, source_ref, map_ref, far_ref, incoming_ref, near_ref, before_ref, out_ref
):
    in_last_chip = lax.axis_index("chip") == 3
    on_first_core = lax.axis_index("core") == 0

    @pl.when(on_first_core & jnp.logical_not(in_last_chip))
    def _():
        incoming = entered(incoming_ref.at[1], near_ref)
        cut(parts(matrix_ref), parts(source_ref), incoming, out_ref)

    @pl.when(on_first_core & in_last_chip)
    def _():
        map_source, map_matrix = parts(map_ref.at[0]), parts(map_ref.at[1])
        incoming = rounded(applied(map_matrix, map_source, parts(far_ref)))
        cut(parts(matrix_ref), parts(source_ref), incoming, out_ref)


def spectra_body(chunks_ref, forward_ref, inverse_ref, weights_ref, out_ref, rows_ref):
    count = chunks_ref.shape[0]
    length = weights_ref.shape[0]
    stride = 2 * ROWS
    rows_ref[...] = chunks_ref[...].astype(F32).reshape(rows_ref.shape)
    taken = [rows_ref[pl.ds(i, count, stride=stride), :].astype(BF16) for i in range(stride)]
    values = jnp.concatenate(
        [jnp.concatenate(taken[:ROWS], axis=1), jnp.concatenate(taken[ROWS:], axis=1)], axis=0
    )
    spectrum = dot(forward_ref[...], values) * (count**-0.5)
    order = [2 * (i % 4) + i // 4 for i in range(ROWS)]
    weights = jnp.concatenate(
        [weights_ref[:, LANES * i : LANES * (i + 1)] for i in order], axis=1
    ).astype(F32)
    real, imag = spectrum[:length], spectrum[length:]
    squared_real = ((real * real - imag * imag) * weights).astype(BF16)
    squared_imag = (2.0 * real * imag * weights).astype(BF16)
    result = dot(inverse_ref[...], jnp.concatenate([squared_real, squared_imag], axis=0))
    result = result * (length**-0.5)
    for i in range(ROWS):
        columns = slice(LANES * i, LANES * (i + 1))
        rows_ref[pl.ds(i, count, stride=stride), :] = result[:count, columns]
        rows_ref[pl.ds(i + ROWS, count, stride=stride), :] = result[count:, columns]
    out_ref[...] = rows_ref[...].reshape(out_ref.shape).astype(BF16)


def output_body(chunks_ref, out_hbm, out_ref, semaphores):
    even = chunks_ref[:, 0].astype(F32)
    odd = chunks_ref[:, 1].astype(F32)
    copies = []
    for part in range(2):
        rows = slice(ROWS * part, ROWS * (part + 1))
        left, right = unchunked(even[:, rows], odd[:, rows])
        value = jnp.concatenate([left, right], axis=1)
        rest = value.shape[0] - ROWS // 2 * FIRST_BACK
        out_ref[part] = jnp.concatenate([value[rest:], value[:rest]], axis=0).astype(BF16)
        copy = pltpu.make_async_copy(out_ref.at[part], out_hbm.at[part], semaphores.at[part])
        copy.start()
        copies.append(copy)
    for copy in copies:
        copy.wait()


def output(chunks, shape):
    return pl.pallas_call(
        output_body,
        out_shape=jax.ShapeDtypeStruct(shape, BF16),
        out_specs=pl.BlockSpec(memory_space=pltpu.HBM),
        scratch_shapes=[pltpu.VMEM(shape, BF16), pltpu.SemaphoreType.DMA((2,))],
        compiler_params=pltpu.CompilerParams(vmem_limit_bytes=24 * 2**20),
        cost_estimate=pl.CostEstimate(flops=0, bytes_accessed=2**19, transcendentals=0),
    )(chunks)


def phase_table(row_count, column_count, length):
    residue = np.arange(row_count)[:, None] * np.arange(column_count)[None, :] % length
    return residue.astype(np.float32) * np.float32(2.0 * math.pi / length)


def complex_table(real, imag):
    return jnp.asarray(np.block([[real, -imag], [imag, real]]).astype(ml_dtypes.bfloat16))


def tables(count, length):
    phase = np.roll(phase_table(length, count, length), -FIRST_OUT, axis=1)
    forward = complex_table(np.cos(phase), -np.sin(phase))
    phase = np.roll(phase_table(count, length, length), -FIRST_BACK, axis=0)
    inverse = complex_table(np.cos(phase), np.sin(phase))
    return forward, inverse


def spectra(chunks, forward, inverse, weights):
    count = chunks.shape[0]
    length = weights.shape[0]
    return pl.pallas_call(
        spectra_body,
        out_shape=jax.ShapeDtypeStruct(chunks.shape, BF16),
        scratch_shapes=[pltpu.VMEM((count * 2 * ROWS, LANES), F32)],
        compiler_params=pltpu.CompilerParams(vmem_limit_bytes=24 * 2**20),
        cost_estimate=pl.CostEstimate(
            flops=16 * length * count * LANES * ROWS, bytes_accessed=3 * 2**18, transcendentals=0
        ),
    )(chunks, forward, inverse, weights)


def after(array, other):
    return lax.optimization_barrier((array, other))[0]


def exchanged(chunks, first):
    count = chunks.shape[0]
    group = [(first + i) % count for i in range(count)]
    return lax.all_to_all(
        chunks, "energy", split_axis=0, concat_axis=0, axis_index_groups=[group], tiled=True
    )


def local(lesser_in, retarded, coupling, interaction):
    order = coupling.shape[-1]
    energies = lax.axis_size("energy")
    shape = (2, order, order)
    chunk = (energies, 2 * ROWS, LANES)
    one = 8 * order**3

    matrix, source, sent = prelude(lesser_in[0, 0], retarded[0, 0], coupling[0])
    sources = lax.all_gather(sent, "core")
    green = call(leading_body, [(shape, BF16)], matrix, source, sources, flops=2 * one)
    arrived = lax.ppermute(green, SPACE, [(1, 3)])
    matrices = lax.all_gather(matrix, "core")
    total, chip_map, weights, forward, inverse = pair_map(
        source,
        sources,
        matrices,
        interaction[0],
        *tables(energies, interaction.shape[1]),
    )
    map_arrived = lax.ppermute(chip_map, SPACE, [(5, 7)])
    green = call(
        hop_body, [(shape, BF16)], chip_map, total, arrived, flops=2 * one
    )
    near = lax.ppermute(green, SPACE, [(3, 5)])
    far = lax.ppermute(green, SPACE, [(3, 7)])
    arrived_later = lax.all_gather(after(arrived, green), "core")
    green = call(
        hop_later_body,
        [(shape, BF16)],
        chip_map,
        total,
        arrived_later,
        flops=2 * one,
    )
    near_later = lax.ppermute(green, SPACE, [(2, 4)])
    far_later = lax.ppermute(green, SPACE, [(2, 6)])
    map_later = lax.ppermute(map_arrived, SPACE, [(7, 6)])
    incoming = call(
        joined_body, [(shape, BF16)], arrived, map_arrived, far, flops=60 * one
    )
    cut_shape = (energies // 2, 2, 2 * ROWS, LANES)
    chunks = call(
        last_body, [(cut_shape, BF16)], chip_map, total, incoming, near, flops=2 * one
    )
    chunks = call(
        last_later_body,
        [(cut_shape, BF16)],
        matrix,
        source,
        map_later,
        far_later,
        arrived_later,
        near_later,
        chunks,
        flops=2 * one,
        in_place=True,
    )
    chunks = exchanged(chunks.reshape(chunk), FIRST_OUT)
    result = spectra(chunks, forward, inverse, weights)
    returned = exchanged(result, FIRST_BACK)
    out = output(returned.reshape(energies // 2, 2, 2 * ROWS, LANES), shape)
    return out.reshape(1, 1, *shape)


def solution(mesh):
    split = Mesh(
        mesh.devices.reshape(mesh.shape["space"] // 2, 2, mesh.shape["energy"]),
        ("chip", "core", "energy"),
    )
    in_specs = (
        P("energy", SPACE, None, None, None),
        P("energy", SPACE, None, None, None),
        P(SPACE, None, None, None),
        P(SPACE, None, "energy"),
    )
    out_specs = P("energy", SPACE, None, None, None)
    return jax.shard_map(local, mesh=split, in_specs=in_specs, out_specs=out_specs, check_vma=False)
```

```python
import functools
import math

import jax
import jax.numpy as jnp
import ml_dtypes
import numpy as np
from jax import lax
from jax.experimental import pallas as pl
from jax.experimental.pallas import tpu as pltpu
from jax.sharding import Mesh
from jax.sharding import PartitionSpec as P

SPACE = ("chip", "core")
BF16 = jnp.bfloat16
F32 = jnp.float32
LANES = 128
ROWS = 8
FIRST_OUT = 46
FIRST_BACK = 34


def dot(left, right):
    return jnp.dot(left, right, preferred_element_type=F32)


def dot_adjoint(left, right):
    return lax.dot_general(left, right, (((1,), (1,)), ((), ())), preferred_element_type=F32)


def product(left, right):
    real_part = dot(
        jnp.concatenate([left[0], -left[1]], axis=1), jnp.concatenate([right[0], right[1]], axis=0)
    )
    imag_part = dot(
        jnp.concatenate([left[0], left[1]], axis=1), jnp.concatenate([right[1], right[0]], axis=0)
    )
    return (real_part, imag_part)


def product_adjoint(left, right):
    right = jnp.concatenate(right, axis=1)
    real_part = dot_adjoint(jnp.concatenate([left[0], left[1]], axis=1), right)
    imag_part = dot_adjoint(jnp.concatenate([left[1], -left[0]], axis=1), right)
    return (real_part, imag_part)


def rounded(pair):
    return (pair[0].astype(BF16), pair[1].astype(BF16))


def parts(ref):
    return (ref[0], ref[1])


def put(ref, pair):
    ref[0] = pair[0].astype(ref.dtype)
    ref[1] = pair[1].astype(ref.dtype)


def applied(matrix, source, green):
    carried = rounded(product(matrix, green))
    grown = product_adjoint(carried, matrix)
    return (source[0] + grown[0], source[1] + grown[1])


def call(body, outs, *operands, flops=0, in_place=False):
    outs = [jax.ShapeDtypeStruct(shape, dtype) for shape, dtype in outs]
    size = sum(math.prod(a.shape) * a.dtype.itemsize for a in [*operands, *outs])
    return pl.pallas_call(
        body,
        out_shape=outs if len(outs) > 1 else outs[0],
        input_output_aliases={len(operands) - 1: 0} if in_place else {},
        compiler_params=pltpu.CompilerParams(vmem_limit_bytes=24 * 2**20),
        cost_estimate=pl.CostEstimate(flops=flops, bytes_accessed=size, transcendentals=0),
    )(*operands)


def prelude_body(
    lesser_hbm, retarded_hbm, coupling_hbm, matrix_ref, source_ref, sent_ref, loaded, semaphores
):
    copies = [
        pltpu.make_async_copy(ref, loaded.at[i], semaphores.at[i])
        for i, ref in enumerate((retarded_hbm, lesser_hbm, coupling_hbm))
    ]
    for copy in copies:
        copy.start()
    copies[0].wait()
    copies[1].wait()
    resolvent = parts(loaded.at[0])
    half = rounded(product(resolvent, parts(loaded.at[1])))
    source = product_adjoint(half, resolvent)
    put(source_ref, source)
    put(sent_ref, source)
    copies[2].wait()
    put(matrix_ref, product(resolvent, parts(loaded.at[2])))


def prelude(lesser_in, retarded, coupling):
    shape = coupling.shape
    return pl.pallas_call(
        prelude_body,
        out_shape=[jax.ShapeDtypeStruct(shape, dtype) for dtype in (BF16, F32, BF16)],
        in_specs=[pl.BlockSpec(memory_space=pltpu.HBM)] * 3,
        out_specs=[pl.BlockSpec(memory_space=pltpu.VMEM)] * 3,
        scratch_shapes=[pltpu.VMEM((3, *shape), BF16), pltpu.SemaphoreType.DMA((3,))],
        compiler_params=pltpu.CompilerParams(vmem_limit_bytes=24 * 2**20),
        cost_estimate=pl.CostEstimate(
            flops=24 * shape[-1] ** 3, bytes_accessed=2**20, transcendentals=0
        ),
    )(*(pltpu.with_memory_space_constraint(a, pltpu.HBM) for a in (lesser_in, retarded, coupling)))


def is_at(**place):
    tests = [lax.axis_index(axis) == index for axis, index in place.items()]
    return functools.reduce(jnp.logical_and, tests)


def leading_body(matrix_ref, source_ref, first_ref, green_ref):
    @pl.when(is_at(chip=0, core=1))
    def _():
        put(green_ref, applied(parts(matrix_ref), parts(source_ref), parts(first_ref.at[0])))


def pair_body(
    source_ref,
    sources_ref,
    matrices_ref,
    weights_hbm,
    forward_hbm,
    inverse_hbm,
    total_ref,
    map_ref,
    weights_ref,
    forward_ref,
    inverse_ref,
    semaphores,
):
    pairs = ((weights_hbm, weights_ref), (forward_hbm, forward_ref), (inverse_hbm, inverse_ref))
    copies = [pltpu.make_async_copy(*pair, semaphores.at[i]) for i, pair in enumerate(pairs)]
    for copy in copies:
        copy.start()

    def composed(second_source):
        second_matrix = parts(matrices_ref.at[1])
        total = applied(second_matrix, second_source, parts(sources_ref.at[0]))
        put(total_ref, total)
        put(map_ref.at[0], total)
        put(map_ref.at[1], product(second_matrix, parts(matrices_ref.at[0])))

    @pl.when(is_at(core=1))
    def _():
        composed(parts(source_ref))

    @pl.when(is_at(core=0))
    def _():
        composed(parts(sources_ref.at[1]))

    for copy in copies:
        copy.wait()


def pair_map(source, sources, matrices, *loads):
    shape = source.shape
    vmem = pl.BlockSpec(memory_space=pltpu.VMEM)
    hbm = pl.BlockSpec(memory_space=pltpu.HBM)
    return pl.pallas_call(
        pair_body,
        out_shape=[
            jax.ShapeDtypeStruct(shape, F32),
            jax.ShapeDtypeStruct((2, *shape), BF16),
            *(jax.ShapeDtypeStruct(a.shape, BF16) for a in loads),
        ],
        in_specs=[vmem] * 3 + [hbm] * 3,
        out_specs=[vmem] * 5,
        scratch_shapes=[pltpu.SemaphoreType.DMA((3,))],
        compiler_params=pltpu.CompilerParams(vmem_limit_bytes=24 * 2**20),
        cost_estimate=pl.CostEstimate(
            flops=24 * shape[-1] ** 3, bytes_accessed=2**20, transcendentals=0
        ),
    )(source, sources, matrices, *(pltpu.with_memory_space_constraint(a, pltpu.HBM) for a in loads))


def hop_body(map_ref, total_ref, arrived_ref, green_ref):
    @pl.when(is_at(chip=1, core=1))
    def _():
        put(green_ref, applied(parts(map_ref.at[1]), parts(total_ref), parts(arrived_ref)))


def hop_later_body(map_ref, total_ref, arrived_ref, green_ref):
    @pl.when(is_at(chip=1, core=0))
    def _():
        put(green_ref, applied(parts(map_ref.at[1]), parts(total_ref), parts(arrived_ref.at[1])))


def joined_body(arrived_ref, map_ref, far_ref, out_ref):
    @pl.when(is_at(chip=3, core=1))
    def _():
        put(out_ref, applied(parts(map_ref.at[1]), parts(map_ref.at[0]), parts(far_ref)))

    @pl.when(lax.axis_index("chip") != 3)
    def _():
        out_ref[...] = arrived_ref[...]


def lower(shape):
    return lax.broadcasted_iota(jnp.int32, shape, 1) < ROWS // 2


def chunked(part):
    left = part[:, :LANES].reshape(-1, ROWS, LANES)
    right = part[:, LANES:].reshape(-1, ROWS, LANES)
    first = lower(left.shape)
    even = jnp.where(first, left, pltpu.roll(right, ROWS // 2, 1))
    odd = jnp.where(first, pltpu.roll(left, ROWS // 2, 1), right)
    return even, odd


def unchunked(even, odd):
    first = lower(even.shape)
    left = jnp.where(first, even, pltpu.roll(odd, ROWS // 2, 1))
    right = jnp.where(first, pltpu.roll(even, ROWS // 2, 1), odd)
    return left.reshape(-1, LANES), right.reshape(-1, LANES)


def rolled(count, start):
    if start == 0:
        return [(slice(0, count), slice(0, count))]
    return [
        (slice(0, count - start), slice(start, count)),
        (slice(count - start, count), slice(0, start)),
    ]


def cut(matrix, source, incoming, out_ref):
    green = applied(matrix, source, incoming)
    even_real, odd_real = chunked(green[0])
    even_imag, odd_imag = chunked(green[1])
    even = jnp.concatenate([even_real, even_imag], axis=1).astype(BF16)
    odd = jnp.concatenate([odd_real, odd_imag], axis=1).astype(BF16)
    for target, taken in rolled(out_ref.shape[0], FIRST_OUT // 2):
        out_ref[target, 0] = even[taken]
        out_ref[target, 1] = odd[taken]


def entered(incoming_ref, near_ref):
    return (incoming_ref[0] + near_ref[0], incoming_ref[1] + near_ref[1])


def last_body(map_ref, total_ref, incoming_ref, near_ref, out_ref):
    @pl.when(is_at(core=1))
    def _():
        incoming = entered(incoming_ref, near_ref)
        cut(parts(map_ref.at[1]), parts(total_ref), incoming, out_ref)


def last_later_body(
    matrix_ref, source_ref, map_ref, far_ref, incoming_ref, near_ref, before_ref, out_ref
):
    in_last_chip = lax.axis_index("chip") == 3
    on_first_core = lax.axis_index("core") == 0

    @pl.when(on_first_core & jnp.logical_not(in_last_chip))
    def _():
        incoming = entered(incoming_ref.at[1], near_ref)
        cut(parts(matrix_ref), parts(source_ref), incoming, out_ref)

    @pl.when(on_first_core & in_last_chip)
    def _():
        map_source, map_matrix = parts(map_ref.at[0]), parts(map_ref.at[1])
        incoming = rounded(applied(map_matrix, map_source, parts(far_ref)))
        cut(parts(matrix_ref), parts(source_ref), incoming, out_ref)


def spectra_body(chunks_ref, forward_ref, inverse_ref, weights_ref, out_ref, rows_ref):
    count = chunks_ref.shape[0]
    length = weights_ref.shape[0]
    stride = 2 * ROWS
    rows_ref[...] = chunks_ref[...].astype(F32).reshape(rows_ref.shape)
    for blocks in ((i, i + 1) for i in range(0, ROWS, 2)):

        def taken(offset):
            rows = [rows_ref[pl.ds(i + offset, count, stride=stride), :] for i in blocks]
            return jnp.concatenate([row.astype(BF16) for row in rows], axis=1)

        values = jnp.concatenate([taken(0), taken(ROWS)], axis=0)
        spectrum = dot(forward_ref[...], values) * (count**-0.5)
        places = [LANES * (2 * (i % 4) + i // 4) for i in blocks]
        weights = [weights_ref[:, at : at + LANES] for at in places]
        weights = jnp.concatenate(weights, axis=1).astype(F32)
        real, imag = spectrum[:length], spectrum[length:]
        squared_real = ((real * real - imag * imag) * weights).astype(BF16)
        squared_imag = (2.0 * real * imag * weights).astype(BF16)
        result = dot(inverse_ref[...], jnp.concatenate([squared_real, squared_imag], axis=0))
        result = result * (length**-0.5)
        for at, i in enumerate(blocks):
            columns = slice(LANES * at, LANES * (at + 1))
            rows_ref[pl.ds(i, count, stride=stride), :] = result[:count, columns]
            rows_ref[pl.ds(i + ROWS, count, stride=stride), :] = result[count:, columns]
    out_ref[...] = rows_ref[...].reshape(out_ref.shape).astype(BF16)


def output_body(chunks_ref, out_hbm, out_ref, semaphores):
    even = chunks_ref[:, 0].astype(F32)
    odd = chunks_ref[:, 1].astype(F32)
    copies = []
    for part in range(2):
        rows = slice(ROWS * part, ROWS * (part + 1))
        left, right = unchunked(even[:, rows], odd[:, rows])
        value = jnp.concatenate([left, right], axis=1)
        rest = value.shape[0] - ROWS // 2 * FIRST_BACK
        out_ref[part] = jnp.concatenate([value[rest:], value[:rest]], axis=0).astype(BF16)
        copy = pltpu.make_async_copy(out_ref.at[part], out_hbm.at[part], semaphores.at[part])
        copy.start()
        copies.append(copy)
    for copy in copies:
        copy.wait()


def output(chunks, shape):
    return pl.pallas_call(
        output_body,
        out_shape=jax.ShapeDtypeStruct(shape, BF16),
        out_specs=pl.BlockSpec(memory_space=pltpu.HBM),
        scratch_shapes=[pltpu.VMEM(shape, BF16), pltpu.SemaphoreType.DMA((2,))],
        compiler_params=pltpu.CompilerParams(vmem_limit_bytes=24 * 2**20),
        cost_estimate=pl.CostEstimate(flops=0, bytes_accessed=2**19, transcendentals=0),
    )(chunks)


def phase_table(row_count, column_count, length):
    residue = np.arange(row_count)[:, None] * np.arange(column_count)[None, :] % length
    return residue.astype(np.float32) * np.float32(2.0 * math.pi / length)


def complex_table(real, imag):
    return jnp.asarray(np.block([[real, -imag], [imag, real]]).astype(ml_dtypes.bfloat16))


def tables(count, length):
    phase = np.roll(phase_table(length, count, length), -FIRST_OUT, axis=1)
    forward = complex_table(np.cos(phase), -np.sin(phase))
    phase = np.roll(phase_table(count, length, length), -FIRST_BACK, axis=0)
    inverse = complex_table(np.cos(phase), np.sin(phase))
    return forward, inverse


def spectra(chunks, forward, inverse, weights):
    count = chunks.shape[0]
    length = weights.shape[0]
    return pl.pallas_call(
        spectra_body,
        out_shape=jax.ShapeDtypeStruct(chunks.shape, BF16),
        scratch_shapes=[pltpu.VMEM((count * 2 * ROWS, LANES), F32)],
        compiler_params=pltpu.CompilerParams(vmem_limit_bytes=24 * 2**20),
        cost_estimate=pl.CostEstimate(
            flops=16 * length * count * LANES * ROWS, bytes_accessed=3 * 2**18, transcendentals=0
        ),
    )(chunks, forward, inverse, weights)


def after(array, other):
    return lax.optimization_barrier((array, other))[0]


def exchanged(chunks, first):
    count = chunks.shape[0]
    group = [(first + i) % count for i in range(count)]
    return lax.all_to_all(
        chunks, "energy", split_axis=0, concat_axis=0, axis_index_groups=[group], tiled=True
    )


def local(lesser_in, retarded, coupling, interaction):
    order = coupling.shape[-1]
    energies = lax.axis_size("energy")
    shape = (2, order, order)
    chunk = (energies, 2 * ROWS, LANES)
    one = 8 * order**3

    matrix, source, sent = prelude(lesser_in[0, 0], retarded[0, 0], coupling[0])
    sources = lax.all_gather(sent, "core")
    green = call(leading_body, [(shape, BF16)], matrix, source, sources, flops=2 * one)
    arrived = lax.ppermute(green, SPACE, [(1, 3)])
    matrices = lax.all_gather(matrix, "core")
    total, chip_map, weights, forward, inverse = pair_map(
        source,
        sources,
        matrices,
        interaction[0],
        *tables(energies, interaction.shape[1]),
    )
    map_arrived = lax.ppermute(chip_map, SPACE, [(5, 7)])
    green = call(
        hop_body, [(shape, BF16)], chip_map, total, arrived, flops=2 * one
    )
    near = lax.ppermute(green, SPACE, [(3, 5)])
    far = lax.ppermute(green, SPACE, [(3, 7)])
    arrived_later = lax.all_gather(after(arrived, green), "core")
    green = call(
        hop_later_body,
        [(shape, BF16)],
        chip_map,
        total,
        arrived_later,
        flops=2 * one,
    )
    near_later = lax.ppermute(green, SPACE, [(2, 4)])
    far_later = lax.ppermute(green, SPACE, [(2, 6)])
    map_later = lax.ppermute(map_arrived, SPACE, [(7, 6)])
    incoming = call(
        joined_body, [(shape, BF16)], arrived, map_arrived, far, flops=60 * one
    )
    cut_shape = (energies // 2, 2, 2 * ROWS, LANES)
    chunks = call(
        last_body, [(cut_shape, BF16)], chip_map, total, incoming, near, flops=2 * one
    )
    chunks = call(
        last_later_body,
        [(cut_shape, BF16)],
        matrix,
        source,
        map_later,
        far_later,
        arrived_later,
        near_later,
        chunks,
        flops=2 * one,
        in_place=True,
    )
    chunks = exchanged(chunks.reshape(chunk), FIRST_OUT)
    result = spectra(chunks, forward, inverse, weights)
    returned = exchanged(result, FIRST_BACK)
    out = output(returned.reshape(energies // 2, 2, 2 * ROWS, LANES), shape)
    return out.reshape(1, 1, *shape)


def solution(mesh):
    split = Mesh(
        mesh.devices.reshape(mesh.shape["space"] // 2, 2, mesh.shape["energy"]),
        ("chip", "core", "energy"),
    )
    in_specs = (
        P("energy", SPACE, None, None, None),
        P("energy", SPACE, None, None, None),
        P(SPACE, None, None, None),
        P(SPACE, None, "energy"),
    )
    out_specs = P("energy", SPACE, None, None, None)
    return jax.shard_map(local, mesh=split, in_specs=in_specs, out_specs=out_specs, check_vma=False)
```

```python
import functools
import math

import jax
import jax.numpy as jnp
import ml_dtypes
import numpy as np
from jax import lax
from jax.experimental import pallas as pl
from jax.experimental.pallas import tpu as pltpu
from jax.sharding import Mesh
from jax.sharding import PartitionSpec as P

SPACE = ("chip", "core")
BF16 = jnp.bfloat16
F32 = jnp.float32
LANES = 128
ROWS = 8
FIRST_OUT = 46
FIRST_BACK = 34


def dot(left, right):
    return jnp.dot(left, right, preferred_element_type=F32)


def dot_adjoint(left, right):
    return lax.dot_general(left, right, (((1,), (1,)), ((), ())), preferred_element_type=F32)


def product(left, right):
    real_part = dot(
        jnp.concatenate([left[0], -left[1]], axis=1), jnp.concatenate([right[0], right[1]], axis=0)
    )
    imag_part = dot(
        jnp.concatenate([left[0], left[1]], axis=1), jnp.concatenate([right[1], right[0]], axis=0)
    )
    return (real_part, imag_part)


def product_adjoint(left, right):
    right = jnp.concatenate(right, axis=1)
    real_part = dot_adjoint(jnp.concatenate([left[0], left[1]], axis=1), right)
    imag_part = dot_adjoint(jnp.concatenate([left[1], -left[0]], axis=1), right)
    return (real_part, imag_part)


def rounded(pair):
    return (pair[0].astype(BF16), pair[1].astype(BF16))


def parts(ref):
    return (ref[0], ref[1])


def put(ref, pair):
    ref[0] = pair[0].astype(ref.dtype)
    ref[1] = pair[1].astype(ref.dtype)


def applied(matrix, source, green):
    carried = rounded(product(matrix, green))
    grown = product_adjoint(carried, matrix)
    return (source[0] + grown[0], source[1] + grown[1])


def call(body, outs, *operands, flops=0, in_place=False):
    outs = [jax.ShapeDtypeStruct(shape, dtype) for shape, dtype in outs]
    size = sum(math.prod(a.shape) * a.dtype.itemsize for a in [*operands, *outs])
    return pl.pallas_call(
        body,
        out_shape=outs if len(outs) > 1 else outs[0],
        input_output_aliases={len(operands) - 1: 0} if in_place else {},
        compiler_params=pltpu.CompilerParams(vmem_limit_bytes=24 * 2**20),
        cost_estimate=pl.CostEstimate(flops=flops, bytes_accessed=size, transcendentals=0),
    )(*operands)


def prelude_body(
    lesser_hbm, retarded_hbm, coupling_hbm, matrix_ref, source_ref, sent_ref, loaded, semaphores
):
    copies = [
        pltpu.make_async_copy(ref, loaded.at[i], semaphores.at[i])
        for i, ref in enumerate((retarded_hbm, lesser_hbm, coupling_hbm))
    ]
    for copy in copies:
        copy.start()
    copies[0].wait()
    copies[1].wait()
    resolvent = parts(loaded.at[0])
    half = rounded(product(resolvent, parts(loaded.at[1])))
    source = product_adjoint(half, resolvent)
    put(source_ref, source)
    put(sent_ref, source)
    copies[2].wait()
    put(matrix_ref, product(resolvent, parts(loaded.at[2])))


def prelude(lesser_in, retarded, coupling):
    shape = coupling.shape
    return pl.pallas_call(
        prelude_body,
        out_shape=[jax.ShapeDtypeStruct(shape, dtype) for dtype in (BF16, F32, BF16)],
        in_specs=[pl.BlockSpec(memory_space=pltpu.HBM)] * 3,
        out_specs=[pl.BlockSpec(memory_space=pltpu.VMEM)] * 3,
        scratch_shapes=[pltpu.VMEM((3, *shape), BF16), pltpu.SemaphoreType.DMA((3,))],
        compiler_params=pltpu.CompilerParams(vmem_limit_bytes=24 * 2**20),
        cost_estimate=pl.CostEstimate(
            flops=24 * shape[-1] ** 3, bytes_accessed=2**20, transcendentals=0
        ),
    )(*(pltpu.with_memory_space_constraint(a, pltpu.HBM) for a in (lesser_in, retarded, coupling)))


def is_at(**place):
    tests = [lax.axis_index(axis) == index for axis, index in place.items()]
    return functools.reduce(jnp.logical_and, tests)


def leading_body(matrix_ref, source_ref, first_ref, green_ref):
    @pl.when(is_at(chip=0, core=1))
    def _():
        put(green_ref, applied(parts(matrix_ref), parts(source_ref), parts(first_ref.at[0])))


def pair_body(
    source_ref,
    sources_ref,
    matrices_ref,
    weights_hbm,
    forward_hbm,
    inverse_hbm,
    total_ref,
    map_ref,
    weights_ref,
    forward_ref,
    inverse_ref,
    semaphores,
):
    pairs = ((weights_hbm, weights_ref), (forward_hbm, forward_ref), (inverse_hbm, inverse_ref))
    copies = [pltpu.make_async_copy(*pair, semaphores.at[i]) for i, pair in enumerate(pairs)]
    for copy in copies:
        copy.start()

    def composed(second_source):
        second_matrix = parts(matrices_ref.at[1])
        total = applied(second_matrix, second_source, parts(sources_ref.at[0]))
        put(total_ref, total)
        put(map_ref.at[0], total)
        put(map_ref.at[1], product(second_matrix, parts(matrices_ref.at[0])))

    @pl.when(is_at(core=1))
    def _():
        composed(parts(source_ref))

    @pl.when(is_at(core=0))
    def _():
        composed(parts(sources_ref.at[1]))

    for copy in copies:
        copy.wait()


def pair_map(source, sources, matrices, *loads):
    shape = source.shape
    vmem = pl.BlockSpec(memory_space=pltpu.VMEM)
    hbm = pl.BlockSpec(memory_space=pltpu.HBM)
    return pl.pallas_call(
        pair_body,
        out_shape=[
            jax.ShapeDtypeStruct(shape, F32),
            jax.ShapeDtypeStruct((2, *shape), BF16),
            *(jax.ShapeDtypeStruct(a.shape, BF16) for a in loads),
        ],
        in_specs=[vmem] * 3 + [hbm] * 3,
        out_specs=[vmem] * 5,
        scratch_shapes=[pltpu.SemaphoreType.DMA((3,))],
        compiler_params=pltpu.CompilerParams(vmem_limit_bytes=24 * 2**20),
        cost_estimate=pl.CostEstimate(
            flops=24 * shape[-1] ** 3, bytes_accessed=2**20, transcendentals=0
        ),
    )(source, sources, matrices, *(pltpu.with_memory_space_constraint(a, pltpu.HBM) for a in loads))


def hop_body(map_ref, total_ref, arrived_ref, green_ref):
    @pl.when(is_at(chip=1, core=1))
    def _():
        put(green_ref, applied(parts(map_ref.at[1]), parts(total_ref), parts(arrived_ref)))


def hop_later_body(map_ref, total_ref, arrived_ref, green_ref):
    @pl.when(is_at(chip=1, core=0))
    def _():
        put(green_ref, applied(parts(map_ref.at[1]), parts(total_ref), parts(arrived_ref.at[1])))


def joined_body(arrived_ref, map_ref, far_ref, out_ref):
    @pl.when(is_at(chip=3, core=1))
    def _():
        put(out_ref, applied(parts(map_ref.at[1]), parts(map_ref.at[0]), parts(far_ref)))

    @pl.when(lax.axis_index("chip") != 3)
    def _():
        out_ref[...] = arrived_ref[...]


def lower(shape):
    return lax.broadcasted_iota(jnp.int32, shape, 1) < ROWS // 2


def chunked(part):
    left = part[:, :LANES].reshape(-1, ROWS, LANES)
    right = part[:, LANES:].reshape(-1, ROWS, LANES)
    first = lower(left.shape)
    even = jnp.where(first, left, pltpu.roll(right, ROWS // 2, 1))
    odd = jnp.where(first, pltpu.roll(left, ROWS // 2, 1), right)
    return even, odd


def unchunked(even, odd):
    first = lower(even.shape)
    left = jnp.where(first, even, pltpu.roll(odd, ROWS // 2, 1))
    right = jnp.where(first, pltpu.roll(even, ROWS // 2, 1), odd)
    return left.reshape(-1, LANES), right.reshape(-1, LANES)


def rolled(count, start):
    if start == 0:
        return [(slice(0, count), slice(0, count))]
    return [
        (slice(0, count - start), slice(start, count)),
        (slice(count - start, count), slice(0, start)),
    ]


def cut(matrix, source, incoming, out_ref):
    green = applied(matrix, source, incoming)
    even_real, odd_real = chunked(green[0])
    even_imag, odd_imag = chunked(green[1])
    even = jnp.concatenate([even_real, even_imag], axis=1).astype(BF16)
    odd = jnp.concatenate([odd_real, odd_imag], axis=1).astype(BF16)
    for target, taken in rolled(out_ref.shape[0], FIRST_OUT // 2):
        out_ref[target, 0] = even[taken]
        out_ref[target, 1] = odd[taken]


def entered(incoming_ref, near_ref):
    return (incoming_ref[0] + near_ref[0], incoming_ref[1] + near_ref[1])


def last_body(map_ref, total_ref, incoming_ref, near_ref, out_ref):
    @pl.when(is_at(core=1))
    def _():
        incoming = entered(incoming_ref, near_ref)
        cut(parts(map_ref.at[1]), parts(total_ref), incoming, out_ref)


def last_later_body(
    matrix_ref, source_ref, map_ref, far_ref, incoming_ref, near_ref, before_ref, out_ref
):
    in_last_chip = lax.axis_index("chip") == 3
    on_first_core = lax.axis_index("core") == 0

    @pl.when(on_first_core & jnp.logical_not(in_last_chip))
    def _():
        incoming = entered(incoming_ref.at[1], near_ref)
        cut(parts(matrix_ref), parts(source_ref), incoming, out_ref)

    @pl.when(on_first_core & in_last_chip)
    def _():
        map_source, map_matrix = parts(map_ref.at[0]), parts(map_ref.at[1])
        incoming = rounded(applied(map_matrix, map_source, parts(far_ref)))
        cut(parts(matrix_ref), parts(source_ref), incoming, out_ref)


def spectra_body(chunks_ref, forward_ref, inverse_ref, weights_ref, out_ref, rows_ref):
    count = chunks_ref.shape[0]
    length = weights_ref.shape[0]
    stride = 2 * ROWS
    rows_ref[...] = chunks_ref[...].astype(F32).reshape(rows_ref.shape)
    taken = [rows_ref[pl.ds(i, count, stride=stride), :].astype(BF16) for i in range(stride)]
    values = jnp.concatenate(
        [jnp.concatenate(taken[:ROWS], axis=1), jnp.concatenate(taken[ROWS:], axis=1)], axis=0
    )
    spectrum = dot(forward_ref[...], values)
    order = [2 * (i % 4) + i // 4 for i in range(ROWS)]
    weights = jnp.concatenate(
        [weights_ref[:, LANES * i : LANES * (i + 1)] for i in order], axis=1
    ).astype(F32)
    real, imag = spectrum[:length], spectrum[length:]
    squared_real = ((real * real - imag * imag) * weights).astype(BF16)
    squared_imag = (2.0 * real * imag * weights).astype(BF16)
    result = dot(inverse_ref[...], jnp.concatenate([squared_real, squared_imag], axis=0))
    result = result * (length**-0.5)
    for i in range(ROWS):
        columns = slice(LANES * i, LANES * (i + 1))
        rows_ref[pl.ds(i, count, stride=stride), :] = result[:count, columns]
        rows_ref[pl.ds(i + ROWS, count, stride=stride), :] = result[count:, columns]
    out_ref[...] = rows_ref[...].reshape(out_ref.shape).astype(BF16)


def output_body(chunks_ref, out_hbm, out_ref, semaphores):
    even = chunks_ref[:, 0].astype(F32)
    odd = chunks_ref[:, 1].astype(F32)
    copies = []
    for part in range(2):
        rows = slice(ROWS * part, ROWS * (part + 1))
        left, right = unchunked(even[:, rows], odd[:, rows])
        value = jnp.concatenate([left, right], axis=1)
        rest = value.shape[0] - ROWS // 2 * FIRST_BACK
        out_ref[part] = jnp.concatenate([value[rest:], value[:rest]], axis=0).astype(BF16)
        copy = pltpu.make_async_copy(out_ref.at[part], out_hbm.at[part], semaphores.at[part])
        copy.start()
        copies.append(copy)
    for copy in copies:
        copy.wait()


def output(chunks, shape):
    return pl.pallas_call(
        output_body,
        out_shape=jax.ShapeDtypeStruct(shape, BF16),
        out_specs=pl.BlockSpec(memory_space=pltpu.HBM),
        scratch_shapes=[pltpu.VMEM(shape, BF16), pltpu.SemaphoreType.DMA((2,))],
        compiler_params=pltpu.CompilerParams(vmem_limit_bytes=24 * 2**20),
        cost_estimate=pl.CostEstimate(flops=0, bytes_accessed=2**19, transcendentals=0),
    )(chunks)


def phase_table(row_count, column_count, length):
    residue = np.arange(row_count)[:, None] * np.arange(column_count)[None, :] % length
    return residue.astype(np.float32) * np.float32(2.0 * math.pi / length)


def complex_table(real, imag):
    return jnp.asarray(np.block([[real, -imag], [imag, real]]).astype(ml_dtypes.bfloat16))


def tables(count, length):
    phase = np.roll(phase_table(length, count, length), -FIRST_OUT, axis=1)
    scale = count**-0.5
    forward = complex_table(scale * np.cos(phase), -scale * np.sin(phase))
    phase = np.roll(phase_table(count, length, length), -FIRST_BACK, axis=0)
    inverse = complex_table(np.cos(phase), np.sin(phase))
    return forward, inverse


def spectra(chunks, forward, inverse, weights):
    count = chunks.shape[0]
    length = weights.shape[0]
    return pl.pallas_call(
        spectra_body,
        out_shape=jax.ShapeDtypeStruct(chunks.shape, BF16),
        scratch_shapes=[pltpu.VMEM((count * 2 * ROWS, LANES), F32)],
        compiler_params=pltpu.CompilerParams(vmem_limit_bytes=24 * 2**20),
        cost_estimate=pl.CostEstimate(
            flops=16 * length * count * LANES * ROWS, bytes_accessed=3 * 2**18, transcendentals=0
        ),
    )(chunks, forward, inverse, weights)


def after(array, other):
    return lax.optimization_barrier((array, other))[0]


def exchanged(chunks, first):
    count = chunks.shape[0]
    group = [(first + i) % count for i in range(count)]
    return lax.all_to_all(
        chunks, "energy", split_axis=0, concat_axis=0, axis_index_groups=[group], tiled=True
    )


def local(lesser_in, retarded, coupling, interaction):
    order = coupling.shape[-1]
    energies = lax.axis_size("energy")
    shape = (2, order, order)
    chunk = (energies, 2 * ROWS, LANES)
    one = 8 * order**3

    matrix, source, sent = prelude(lesser_in[0, 0], retarded[0, 0], coupling[0])
    sources = lax.all_gather(sent, "core")
    green = call(leading_body, [(shape, BF16)], matrix, source, sources, flops=2 * one)
    arrived = lax.ppermute(green, SPACE, [(1, 3)])
    matrices = lax.all_gather(matrix, "core")
    total, chip_map, weights, forward, inverse = pair_map(
        source,
        sources,
        matrices,
        interaction[0],
        *tables(energies, interaction.shape[1]),
    )
    map_arrived = lax.ppermute(chip_map, SPACE, [(5, 7)])
    green = call(
        hop_body, [(shape, BF16)], chip_map, total, arrived, flops=2 * one
    )
    near = lax.ppermute(green, SPACE, [(3, 5)])
    far = lax.ppermute(green, SPACE, [(3, 7)])
    arrived_later = lax.all_gather(after(arrived, green), "core")
    green = call(
        hop_later_body,
        [(shape, BF16)],
        chip_map,
        total,
        arrived_later,
        flops=2 * one,
    )
    near_later = lax.ppermute(green, SPACE, [(2, 4)])
    far_later = lax.ppermute(green, SPACE, [(2, 6)])
    map_later = lax.ppermute(map_arrived, SPACE, [(7, 6)])
    incoming = call(
        joined_body, [(shape, BF16)], arrived, map_arrived, far, flops=60 * one
    )
    cut_shape = (energies // 2, 2, 2 * ROWS, LANES)
    chunks = call(
        last_body, [(cut_shape, BF16)], chip_map, total, incoming, near, flops=2 * one
    )
    chunks = call(
        last_later_body,
        [(cut_shape, BF16)],
        matrix,
        source,
        map_later,
        far_later,
        arrived_later,
        near_later,
        chunks,
        flops=2 * one,
        in_place=True,
    )
    chunks = exchanged(chunks.reshape(chunk), FIRST_OUT)
    result = spectra(chunks, forward, inverse, weights)
    returned = exchanged(result, FIRST_BACK)
    out = output(returned.reshape(energies // 2, 2, 2 * ROWS, LANES), shape)
    return out.reshape(1, 1, *shape)


def solution(mesh):
    split = Mesh(
        mesh.devices.reshape(mesh.shape["space"] // 2, 2, mesh.shape["energy"]),
        ("chip", "core", "energy"),
    )
    in_specs = (
        P("energy", SPACE, None, None, None),
        P("energy", SPACE, None, None, None),
        P(SPACE, None, None, None),
        P(SPACE, None, "energy"),
    )
    out_specs = P("energy", SPACE, None, None, None)
    return jax.shard_map(local, mesh=split, in_specs=in_specs, out_specs=out_specs, check_vma=False)
```
